512 devices in a mesh: rows: 64 (over z, y), cols: 8 (over x, core).
Axes of the slice: x: 4, y: 4, z: 16, core: 2. Of those that a mesh axis runs over, the one named last changes fastest.
Arguments:
- block_vector: float32 [524288, 128], P('rows'), may hold values from -6 to 6
- op_tiles: float32 [4096, 8, 128, 128], P('rows', 'cols')
- tile_cols: int32 [4096, 8], P('rows', 'cols'), may hold values from 0 to 4095, as said below
- live_counts: int32 [4096], P('rows'), may hold values from 1 to 8
Outputs:
- basis_block: float32 [524288, 128], P(('rows', 'cols'))
- r_factor: float32 [128, 128], replicated
The draws below stay inside these ranges and needn't reach their ends.
Inputs may be any that keep to these rules, and one draw needn't show every extreme that they name: `tile_cols`: slot 0 of row block i names i itself. Every entry names a row block of the same index of rows as i, or of the index just before or after it.
All inputs are finite; a program needn't handle non-finite values.
Results may differ from the reference program's by a relative error of at most 0.0003.
Values sent between devices are 32-bit elements; how exact they have to be, the bound alone decides.
No kernel may reach another device: no remote copies, remote signals or barrier semaphores. Data moves between devices by JAX's collectives and lax.ppermute only.
A program may use at most 128 MiB of HBM per device.

```python
import jax
import jax.numpy as jnp
from jax import lax

RB_DEV = 64
TILE = 128
BW = 128
K = 8
NB = 4096
NODES = 524288


def draw_op_tiles(key, part):
    key = jax.random.fold_in(key, 11)
    key_off, key_diag = jax.random.split(key)
    off_part = jax.random.normal(key_off, (NB, K, TILE, TILE), jnp.float32) * 0.08
    top_log = jnp.log(10.0)
    uniform_draw = jax.random.uniform(key_diag, (NB, TILE), jnp.float32)
    rising = 1.0 + 2.0 * jnp.arange(NB, dtype=jnp.float32) / NB
    diag_vals = jnp.exp(uniform_draw * top_log) * rising[:, None]
    diag_tiles = diag_vals[:, :, None] * jnp.eye(TILE, dtype=jnp.float32)[None, :, :]
    return off_part.at[:, 0].add(diag_tiles)


def draw_tile_cols(key, part):
    key = jax.random.fold_in(key, 7)
    row_ids = jnp.arange(NB, dtype=jnp.int32)
    owner = row_ids // RB_DEV
    offsets = jax.random.randint(key, (NB, K), 0, 3 * RB_DEV, dtype=jnp.int32)
    targets = jnp.clip(owner[:, None] * RB_DEV - RB_DEV + offsets, 0, NB - 1)
    return targets.at[:, 0].set(row_ids).astype(jnp.int32)


def draw_live_counts(key, part):
    key = jax.random.fold_in(key, 5)
    counts_drawn = jax.random.randint(key, (NB,), 1, K + 1, dtype=jnp.int32)
    return counts_drawn.at[0].set(K).at[NB - 1].set(1).astype(jnp.int32)


def block_levels(rng, shape, shards, least, largest):
    factor_of = 1.0
    for axis_at, parts in shards:
        steps = jax.random.uniform(jax.random.fold_in(jax.random.fold_in(rng, 6), axis_at), (parts,), jnp.float32, least / len(shards), largest / len(shards))
        factor_of = factor_of * jnp.repeat(jnp.exp(steps), shape[axis_at] // parts).reshape((-1,) + (1,) * (len(shape) - 1 - axis_at))
    return factor_of


def bell_draw(own_key, dims, scale, limit, shards=(), kind=jnp.bfloat16):
    array = jax.random.normal(own_key, dims, jnp.float32) * scale
    if len(shards) > 0:
        array = block_levels(own_key, dims, shards, -0.22, 0.18) * array
    return jnp.clip(array, min=-limit, max=limit).astype(kind)


def setup_inputs(seed: int = 0) -> dict:
    keys = jax.random.split(jax.random.key(seed), 5)
    return {
        "block_vector": bell_draw(keys[0], (NODES, BW), 1.0, 6.0, ((0, 64),), jnp.float32),
        "op_tiles": draw_op_tiles(jax.random.fold_in(keys[4], 71), 0),
        "tile_cols": draw_tile_cols(jax.random.fold_in(keys[4], 71), 0),
        "live_counts": draw_live_counts(jax.random.fold_in(keys[4], 71), 0),
    }


def reference(block_vector, op_tiles, tile_cols, live_counts):
    vec_blocks = block_vector.reshape(NB, TILE, BW)
    slot_ids = jnp.arange(K, dtype=jnp.int32)

    def row_block(items):
        tiles_row, cols_row, count_row = items
        live_mask = (slot_ids < count_row).astype(jnp.float32)
        picked = vec_blocks[cols_row] * live_mask[:, None, None]
        return jnp.einsum('sab,sbc->ac', tiles_row, picked, precision=lax.Precision.HIGHEST)
    product = lax.map(row_block, (op_tiles, tile_cols, live_counts)).reshape(NODES, BW)
    gram_matrix = jnp.einsum('ra,rb->ab', product, product, precision=lax.Precision.HIGHEST)
    chol_lower = jnp.linalg.cholesky(gram_matrix)
    solved = jax.scipy.linalg.solve_triangular(chol_lower, product.T, lower=True)
    root_nodes = jnp.sqrt(jnp.float32(NODES))
    return (solved.T * root_nodes, chol_lower.T / root_nodes)
```

```python
import functools
import itertools

import jax
import jax.numpy as jnp
from jax import lax
from jax.experimental import pallas as pl
from jax.experimental.pallas import tpu as pltpu
from jax.sharding import PartitionSpec as P

EXACT = lax.Precision.HIGHEST
SUBLANES = 8


def split_bf16(x):
    high = x.astype(jnp.bfloat16)
    low = (x - high.astype(jnp.float32)).astype(jnp.bfloat16)
    return high, low


def product_kernel(
    idx_ref, count_ref, place_ref, own_ref, left_ref, left_other_ref, right_ref, right_other_ref, tile_ref,
    out_ref, gram_ref, tile_buf, vec_buf, tile_sem, vec_sem,
):
    slots, rows_kept, size, width = tile_ref.shape
    blocks = own_ref.shape[0] // size
    half = blocks // 2
    first_row, core = place_ref[0], place_ref[1]

    def copy_vec(source, block, at):
        start = pl.multiple_of(block * size, size)
        return pltpu.make_async_copy(source.at[pl.ds(start, size)], vec_buf.at[at], vec_sem.at[at])

    def fetch(at, carry):
        row, slot = at // slots, at % slots
        pltpu.make_async_copy(tile_ref.at[slot, row], tile_buf.at[at], tile_sem.at[at]).start()
        block = idx_ref[slot, row]
        side, within = block // blocks, block % blocks
        first_half = within // half == core
        place = within % half

        @pl.when(side == 1)
        def _():
            copy_vec(own_ref, within, at).start()

        @pl.when((side == 0) & first_half)
        def _():
            copy_vec(left_ref, place, at).start()

        @pl.when((side == 0) & jnp.logical_not(first_half))
        def _():
            copy_vec(left_other_ref, place, at).start()

        @pl.when((side == 2) & first_half)
        def _():
            copy_vec(right_ref, place, at).start()

        @pl.when((side == 2) & jnp.logical_not(first_half))
        def _():
            copy_vec(right_other_ref, place, at).start()

        return carry

    lax.fori_loop(0, slots * rows_kept, fetch, 0)
    gram_ref[...] = jnp.zeros_like(gram_ref)

    def row_block(row, carry):
        count = count_ref[first_row + row]
        total = jnp.zeros((size, width), jnp.float32)
        for slot in range(0, slots, 2):
            tiles, vecs = [], []
            for one in (slot, slot + 1):
                at = row * slots + one
                pltpu.make_async_copy(tile_ref.at[one, row], tile_buf.at[at], tile_sem.at[at]).wait()
                copy_vec(own_ref, 0, at).wait()
                tiles.append(tile_buf[at])
                vecs.append(vec_buf[at] * (one < count).astype(jnp.float32))
            tile_high, tile_low = split_bf16(jnp.concatenate(tiles, axis=1))
            vec_high, vec_low = split_bf16(jnp.concatenate(vecs, axis=0))
            both = jnp.dot(
                tile_high, jnp.concatenate([vec_high, vec_low], axis=1), preferred_element_type=jnp.float32
            )
            total += both[:, :width] + both[:, width:]
            total += jnp.dot(tile_low, vec_high, preferred_element_type=jnp.float32)
        out_ref[pl.ds(pl.multiple_of(row * size, size), size), :] = total
        gram_ref[...] += lax.dot_general(
            total, total, (((0,), (0,)), ((), ())), precision=EXACT, preferred_element_type=jnp.float32
        )
        return carry

    lax.fori_loop(0, rows_kept, row_block, 0)


def product_and_gram(idx, counts, place, own, left, left_other, right, right_other, tiles):
    slots, rows_kept, size, width = tiles.shape
    held = slots * rows_kept
    in_smem = pl.BlockSpec(memory_space=pltpu.SMEM)
    in_vmem = pl.BlockSpec(memory_space=pltpu.VMEM)
    anywhere = pl.BlockSpec(memory_space=pl.ANY)
    return pl.pallas_call(
        product_kernel,
        out_shape=(
            jax.ShapeDtypeStruct((rows_kept * size, width), jnp.float32),
            jax.ShapeDtypeStruct((width, width), jnp.float32),
        ),
        in_specs=[in_smem] * 3 + [anywhere] * 6,
        out_specs=(in_vmem, in_vmem),
        scratch_shapes=[
            pltpu.VMEM((held, size, size), jnp.float32),
            pltpu.VMEM((held, size, width), jnp.float32),
            pltpu.SemaphoreType.DMA((held,)),
            pltpu.SemaphoreType.DMA((held,)),
        ],
        compiler_params=pltpu.CompilerParams(vmem_limit_bytes=24 << 20),
    )(idx, counts, place, own, left, left_other, right, right_other, tiles)


def factor_kernel(nodes, gram_ref, rows_ref, basis_ref, factor_ref):
    size = gram_ref.shape[0]
    groups = size // SUBLANES
    gram = [gram_ref[SUBLANES * i : SUBLANES * (i + 1), :] for i in range(groups)]
    lane = lax.broadcasted_iota(jnp.int32, (SUBLANES, size), 1)
    sub = lax.broadcasted_iota(jnp.int32, (SUBLANES, size), 0)
    inverse = [(lane == sub + SUBLANES * i).astype(jnp.float32) for i in range(groups)]
    for step in range(size):
        group, within = divmod(step, SUBLANES)
        pivot_row = jnp.broadcast_to(gram[group][within : within + 1, :], (SUBLANES, size))
        inverse_row = jnp.broadcast_to(inverse[group][within : within + 1, :], (SUBLANES, size))
        scale = 1.0 / jnp.broadcast_to(pivot_row[:, step : step + 1], (SUBLANES, size))
        pivot_row, inverse_row = pivot_row * scale, inverse_row * scale
        for other in range(group, groups):
            if other == group and within == SUBLANES - 1:
                continue
            factor = jnp.broadcast_to(gram[other][:, step : step + 1], (SUBLANES, size))
            if other == group:
                factor = jnp.where(sub > within, factor, 0.0)
            gram[other] = gram[other] - factor * pivot_row
            inverse[other] = inverse[other] - factor * inverse_row
    root = jnp.sqrt(jnp.float32(nodes))
    for group in range(groups):
        here = sub + SUBLANES * group
        diagonal = jnp.sum(jnp.where(lane == here, gram[group], 0.0), axis=1, keepdims=True)
        scale = lax.rsqrt(diagonal)
        factor_ref[SUBLANES * group : SUBLANES * (group + 1), :] = jnp.where(lane >= here, gram[group] * scale, 0.0) / root
        inverse[group] = inverse[group] * (scale * root)
    basis_ref[...] = lax.dot_general(
        rows_ref[...], jnp.concatenate(inverse, axis=0), (((1,), (1,)), ((), ())),
        precision=EXACT, preferred_element_type=jnp.float32,
    )


def basis_and_factor(nodes, gram, rows):
    in_vmem = pl.BlockSpec(memory_space=pltpu.VMEM)
    return pl.pallas_call(
        functools.partial(factor_kernel, nodes),
        out_shape=(jax.ShapeDtypeStruct(rows.shape, jnp.float32), jax.ShapeDtypeStruct(gram.shape, jnp.float32)),
        in_specs=[in_vmem] * 2,
        out_specs=(in_vmem, in_vmem),
        compiler_params=pltpu.CompilerParams(vmem_limit_bytes=24 << 20),
    )(gram, rows)


def device_groups(row_devices, col_devices, row_step, key):
    groups = {}
    for row, col in itertools.product(range(row_devices), range(col_devices)):
        groups.setdefault(key(row // row_step, row % row_step, col), []).append(row * col_devices + col)
    return list(groups.values())


def exchange(pieces, groups):
    return lax.all_to_all(pieces, ("rows", "cols"), 0, 0, axis_index_groups=groups, tiled=True)


def sum_over_devices(gram, row_devices, col_devices):
    row_step = 4
    plane = device_groups(row_devices, col_devices, row_step, lambda z, y, col: z)
    across = device_groups(row_devices, col_devices, row_step, lambda z, y, col: (y, col))
    in_plane, planes = len(plane[0]), len(across[0])
    size, width = gram.shape
    piece = exchange(gram.reshape(in_plane, size // in_plane, width), plane).sum(0)
    piece = exchange(jnp.broadcast_to(piece[None], (planes,) + piece.shape), across).sum(0)
    return exchange(jnp.broadcast_to(piece[None], (in_plane,) + piece.shape), plane).reshape(size, width)


def on_device(block_vector, op_tiles, tile_cols, live_counts):
    block_count, _, size, width = op_tiles.shape
    row_devices, col_devices = lax.axis_size("rows"), lax.axis_size("cols")
    row, col = lax.axis_index("rows"), lax.axis_index("cols")
    rows_here = block_count * size
    rows_kept = block_count // col_devices
    core = col % 2

    def swap(x):
        return lax.ppermute(x, "cols", [(i, i ^ 1) for i in range(col_devices)])

    ends = row_devices - 1
    half = lax.dynamic_slice_in_dim(block_vector, core * (rows_here // 2), rows_here // 2, axis=0)
    left = lax.ppermute(half, "rows", [(i, i + 1) for i in range(ends)])
    right = lax.ppermute(half, "rows", [(i + 1, i) for i in range(ends)])
    tiles = lax.all_to_all(op_tiles.reshape(col_devices, rows_kept, size, size), "cols", 0, 0, tiled=True)
    local_idx = tile_cols - (row - 1) * block_count
    idx = lax.all_to_all(local_idx.reshape(col_devices, rows_kept), "cols", 0, 0, tiled=True)
    place = jnp.stack([col * rows_kept, core]).astype(jnp.int32)
    part_rows, gram = product_and_gram(
        idx, live_counts, place, block_vector, left, swap(left), right, swap(right), tiles
    )
    gram = sum_over_devices(gram, row_devices, col_devices)
    return basis_and_factor(rows_here * row_devices, gram, part_rows)


def solution(mesh):
    in_specs = (P("rows", None), P("rows", "cols", None, None), P("rows", "cols"), P("rows"))
    out_specs = (P(("rows", "cols"), None), P())
    return jax.shard_map(
        on_device, mesh=mesh, in_specs=in_specs, out_specs=out_specs, check_vma=False
    )
```

```python
import functools
import itertools

import jax
import jax.numpy as jnp
from jax import lax
from jax.experimental import pallas as pl
from jax.experimental.pallas import tpu as pltpu
from jax.sharding import PartitionSpec as P

EXACT = lax.Precision.HIGHEST
SUBLANES = 8
PARTS = 2


def split_bf16(x):
    high = x.astype(jnp.bfloat16)
    low = (x - high.astype(jnp.float32)).astype(jnp.bfloat16)
    return high, low


def product_kernel(
    idx_ref, count_ref, place_ref, own_ref, *refs,
):
    near_refs, far_refs = refs[:PARTS], refs[PARTS : 2 * PARTS]
    tile_ref, out_ref, gram_ref, tile_buf, vec_buf, tile_sem, vec_sem = refs[2 * PARTS :]
    slots, rows_kept, size, width = tile_ref.shape
    blocks = own_ref.shape[0] // size
    part = blocks // PARTS
    col, near_side = place_ref[0], place_ref[1]
    first_row = col * rows_kept

    def copy_tiles(row):
        return pltpu.make_async_copy(tile_ref.at[:, row], tile_buf.at[row], tile_sem.at[row])

    def copy_vec(source, block, row, slot):
        start = pl.multiple_of(block * size, size)
        return pltpu.make_async_copy(source.at[pl.ds(start, size)], vec_buf.at[row, slot], vec_sem.at[row, slot])

    def fetch(row, carry):
        copy_tiles(row).start()

        def fetch_vec(slot, inner):
            block = idx_ref[slot, first_row + row]
            side, within = block // blocks, block % blocks
            number, place = within // part, within % part

            @pl.when(side == 1)
            def _():
                copy_vec(own_ref, within, row, slot).start()

            @pl.when(side != 1)
            def _():
                for at in range(PARTS):

                    @pl.when((side == near_side) & (number == at))
                    def _():
                        copy_vec(near_refs[at], place, row, slot).start()

                    @pl.when((side != near_side) & (number == at))
                    def _():
                        copy_vec(far_refs[at], place, row, slot).start()

            return inner

        return lax.fori_loop(0, count_ref[first_row + row], fetch_vec, carry)

    lax.fori_loop(0, rows_kept, fetch, 0)

    def row_block(row, carry):
        count = count_ref[first_row + row]
        copy_tiles(row).wait()

        def wait_vec(slot, inner):
            copy_vec(own_ref, 0, row, slot).wait()
            return inner

        lax.fori_loop(0, count, wait_vec, 0)
        total = jnp.zeros((size, width), jnp.float32)
        for slot in range(0, slots, 2):
            pair = (slot, slot + 1)
            tiles = [tile_buf[row, one] for one in pair]
            vecs = [jnp.where(one < count, vec_buf[row, one], 0.0) for one in pair]
            tile_high, tile_low = split_bf16(jnp.concatenate(tiles, axis=1))
            vec_high, vec_low = split_bf16(jnp.concatenate(vecs, axis=0))
            both = jnp.dot(
                tile_high, jnp.concatenate([vec_high, vec_low], axis=1), preferred_element_type=jnp.float32
            )
            total += both[:, :width] + both[:, width:]
            total += jnp.dot(tile_low, vec_high, preferred_element_type=jnp.float32)
        out_ref[pl.ds(pl.multiple_of(row * size, size), size), :] = total
        return carry

    lax.fori_loop(0, rows_kept, row_block, 0)
    high, low = split_bf16(out_ref[...])
    both = jnp.concatenate([high, low], axis=1)
    gram = lax.dot_general(both, both, (((0,), (0,)), ((), ())), preferred_element_type=jnp.float32)
    gram_ref[...] = gram[:width, :width] + (gram[:width, width:] + gram[width:, :width]) + gram[width:, width:]


def product_and_gram(idx, counts, place, own, near, far, tiles):
    slots, rows_kept, size, width = tiles.shape
    in_smem = pl.BlockSpec(memory_space=pltpu.SMEM)
    in_vmem = pl.BlockSpec(memory_space=pltpu.VMEM)
    anywhere = pl.BlockSpec(memory_space=pl.ANY)
    return pl.pallas_call(
        product_kernel,
        out_shape=(
            jax.ShapeDtypeStruct((rows_kept * size, width), jnp.float32),
            jax.ShapeDtypeStruct((width, width), jnp.float32),
        ),
        in_specs=[in_smem] * 3 + [anywhere] * (2 + 2 * PARTS),
        out_specs=(in_vmem, in_vmem),
        scratch_shapes=[
            pltpu.VMEM((rows_kept, slots, size, size), jnp.float32),
            pltpu.VMEM((rows_kept, slots, size, width), jnp.float32),
            pltpu.SemaphoreType.DMA((rows_kept,)),
            pltpu.SemaphoreType.DMA((rows_kept, slots)),
        ],
        compiler_params=pltpu.CompilerParams(vmem_limit_bytes=62 << 20),
    )(idx, counts, place, own, *near, *far, tiles)


def factor_kernel(nodes, gram_ref, rows_ref, basis_ref, factor_ref):
    size = gram_ref.shape[0]
    groups = size // SUBLANES
    gram = [gram_ref[SUBLANES * i : SUBLANES * (i + 1), :] for i in range(groups)]
    lane = lax.broadcasted_iota(jnp.int32, (SUBLANES, size), 1)
    sub = lax.broadcasted_iota(jnp.int32, (SUBLANES, size), 0)
    inverse = [(lane == sub + SUBLANES * i).astype(jnp.float32) for i in range(groups)]
    for step in range(size):
        group, within = divmod(step, SUBLANES)
        pivot_row = jnp.broadcast_to(gram[group][within : within + 1, :], (SUBLANES, size))
        inverse_row = jnp.broadcast_to(inverse[group][within : within + 1, :], (SUBLANES, size))
        scale = 1.0 / jnp.broadcast_to(pivot_row[:, step : step + 1], (SUBLANES, size))
        pivot_row, inverse_row = pivot_row * scale, inverse_row * scale
        for other in range(group, groups):
            if other == group and within == SUBLANES - 1:
                continue
            factor = jnp.broadcast_to(gram[other][:, step : step + 1], (SUBLANES, size))
            if other == group:
                factor = jnp.where(sub > within, factor, 0.0)
            gram[other] = gram[other] - factor * pivot_row
            inverse[other] = inverse[other] - factor * inverse_row
    root = jnp.sqrt(jnp.float32(nodes))
    for group in range(groups):
        here = sub + SUBLANES * group
        diagonal = jnp.sum(jnp.where(lane == here, gram[group], 0.0), axis=1, keepdims=True)
        scale = lax.rsqrt(diagonal)
        factor_ref[SUBLANES * group : SUBLANES * (group + 1), :] = jnp.where(lane >= here, gram[group] * scale, 0.0) / root
        inverse[group] = inverse[group] * (scale * root)
    basis_ref[...] = lax.dot_general(
        rows_ref[...], jnp.concatenate(inverse, axis=0), (((1,), (1,)), ((), ())),
        precision=EXACT, preferred_element_type=jnp.float32,
    )


def basis_and_factor(nodes, gram, rows):
    in_vmem = pl.BlockSpec(memory_space=pltpu.VMEM)
    return pl.pallas_call(
        functools.partial(factor_kernel, nodes),
        out_shape=(jax.ShapeDtypeStruct(rows.shape, jnp.float32), jax.ShapeDtypeStruct(gram.shape, jnp.float32)),
        in_specs=[in_vmem] * 2,
        out_specs=(in_vmem, in_vmem),
        compiler_params=pltpu.CompilerParams(vmem_limit_bytes=62 << 20),
    )(gram, rows)


def device_groups(row_devices, col_devices, row_step, key):
    groups = {}
    for row, col in itertools.product(range(row_devices), range(col_devices)):
        groups.setdefault(key(row // row_step, row % row_step, col), []).append(row * col_devices + col)
    return list(groups.values())


def exchange(pieces, groups):
    return lax.all_to_all(pieces, ("rows", "cols"), 0, 0, axis_index_groups=groups, tiled=True)


def sum_over_devices(gram, row_devices, col_devices):
    row_step = 4
    plane = device_groups(row_devices, col_devices, row_step, lambda z, y, col: z)
    across = device_groups(row_devices, col_devices, row_step, lambda z, y, col: (y, col))
    in_plane, planes = len(plane[0]), len(across[0])
    size, width = gram.shape
    piece = exchange(gram.reshape(in_plane, size // in_plane, width), plane).sum(0)
    piece = exchange(jnp.broadcast_to(piece[None], (planes,) + piece.shape), across).sum(0)
    return exchange(jnp.broadcast_to(piece[None], (in_plane,) + piece.shape), plane).reshape(size, width)


def on_device(block_vector, op_tiles, tile_cols, live_counts):
    block_count, _, size, width = op_tiles.shape
    row_devices, col_devices = lax.axis_size("rows"), lax.axis_size("cols")
    row, col = lax.axis_index("rows"), lax.axis_index("cols")
    rows_here = block_count * size
    rows_kept = block_count // col_devices
    near_side = 2 * (col % 2)

    def fetched_by(r, c):
        if c % 2 == 0:
            return (r, c + 1) if r == row_devices - 1 else (r + 1, c)
        return (r, c - 1) if r == 0 else (r - 1, c)

    steps = []
    for r, c in itertools.product(range(row_devices), range(col_devices)):
        to_r, to_c = fetched_by(r, c)
        steps.append((r * col_devices + c, to_r * col_devices + to_c))
    rows_part = rows_here // PARTS
    near = [
        lax.ppermute(block_vector[at * rows_part : (at + 1) * rows_part], ("rows", "cols"), steps) for at in range(PARTS)
    ]
    idx = lax.all_gather((tile_cols - (row - 1) * block_count).reshape(block_count), "cols")
    head = jnp.where(jnp.min(idx) < 0, 0.0, near[-1][:SUBLANES])
    near[-1] = lax.dynamic_update_slice(near[-1], head, (0, 0))
    far = [lax.ppermute(part, "cols", [(i, i ^ 1) for i in range(col_devices)]) for part in near]
    tiles = lax.all_to_all(op_tiles.reshape(col_devices, rows_kept, size, size), "cols", 0, 0, tiled=True)
    place = jnp.stack([col, near_side]).astype(jnp.int32)
    part_rows, gram = product_and_gram(idx, live_counts, place, block_vector, near, far, tiles)
    gram = sum_over_devices(gram, row_devices, col_devices)
    return basis_and_factor(rows_here * row_devices, gram, part_rows)


def solution(mesh):
    in_specs = (P("rows", None), P("rows", "cols", None, None), P("rows", "cols"), P("rows"))
    out_specs = (P(("rows", "cols"), None), P())
    return jax.shard_map(
        on_device, mesh=mesh, in_specs=in_specs, out_specs=out_specs, check_vma=False
    )
```

```python
import functools
import itertools

import jax
import jax.numpy as jnp
from jax import lax
from jax.experimental import pallas as pl
from jax.experimental.pallas import tpu as pltpu
from jax.sharding import PartitionSpec as P

EXACT = lax.Precision.HIGHEST
SUBLANES = 8
PARTS = 2


def split_bf16(x):
    high = x.astype(jnp.bfloat16)
    low = (x - high.astype(jnp.float32)).astype(jnp.bfloat16)
    return high, low


def product_kernel(
    count_ref, own_ref, sent_ref, *refs,
):
    near_refs, far_refs = refs[:PARTS], refs[PARTS : 2 * PARTS]
    out_ref, gram_ref, note_buf, tile_buf, vec_buf, note_sem, tile_sem, vec_sem = refs[2 * PARTS :]
    slots = sent_ref.shape[0]
    size, width = tile_buf.shape[2:]
    rows_kept = out_ref.shape[0] // size
    blocks = own_ref.shape[0] // size
    part = blocks // PARTS

    def copy_tiles(row):
        start = pl.multiple_of(row * size, size)
        return pltpu.make_async_copy(sent_ref.at[:, pl.ds(start, size)], tile_buf.at[row], tile_sem.at[row])

    def copy_vec(source, block, row, slot):
        start = pl.multiple_of(block * size, size)
        return pltpu.make_async_copy(source.at[pl.ds(start, size)], vec_buf.at[row, slot], vec_sem.at[row, slot])

    notes = pltpu.make_async_copy(sent_ref.at[:, pl.ds(rows_kept * size, SUBLANES)], note_buf, note_sem)
    notes.start()
    copy_tiles(0).start()
    notes.wait()
    col = note_buf[0, 0, rows_kept].astype(jnp.int32)
    first_row, near_side = col * rows_kept, 2 * (col % 2)

    def fetch(row, carry):
        @pl.when(row > 0)
        def _():
            copy_tiles(row).start()

        def fetch_vec(slot, inner):
            block = note_buf[slot, 0, row].astype(jnp.int32)
            side, within = block // blocks, block % blocks

            @pl.when(side == 1)
            def _():
                copy_vec(own_ref, within, row, slot).start()

            @pl.when(side != 1)
            def _():
                number, place = within // part, within % part
                for at in range(PARTS):

                    @pl.when((side == near_side) & (number == at))
                    def _():
                        copy_vec(near_refs[at], place, row, slot).start()

                    @pl.when((side != near_side) & (number == at))
                    def _():
                        copy_vec(far_refs[at], place, row, slot).start()

            return inner

        return lax.fori_loop(0, count_ref[first_row + row], fetch_vec, carry)

    lax.fori_loop(0, rows_kept, fetch, 0)

    def row_block(row, carry):
        count = count_ref[first_row + row]
        copy_tiles(row).wait()

        def wait_vec(slot, inner):
            copy_vec(own_ref, 0, row, slot).wait()
            return inner

        lax.fori_loop(0, count, wait_vec, 0)
        total = jnp.zeros((size, width), jnp.float32)
        for slot in range(0, slots, 2):
            pair = (slot, slot + 1)
            tiles = [tile_buf[row, one] for one in pair]
            vecs = [jnp.where(one < count, vec_buf[row, one], 0.0) for one in pair]
            tile_high, tile_low = split_bf16(jnp.concatenate(tiles, axis=1))
            vec_high, vec_low = split_bf16(jnp.concatenate(vecs, axis=0))
            both = jnp.dot(
                tile_high, jnp.concatenate([vec_high, vec_low], axis=1), preferred_element_type=jnp.float32
            )
            total += both[:, :width] + both[:, width:]
            total += jnp.dot(tile_low, vec_high, preferred_element_type=jnp.float32)
        out_ref[pl.ds(pl.multiple_of(row * size, size), size), :] = total
        return carry

    lax.fori_loop(0, rows_kept, row_block, 0)
    high, low = split_bf16(out_ref[...])
    both = jnp.concatenate([high, low], axis=1)
    gram = lax.dot_general(both, both, (((0,), (0,)), ((), ())), preferred_element_type=jnp.float32)
    gram_ref[...] = gram[:width, :width] + (gram[:width, width:] + gram[width:, :width]) + gram[width:, width:]


def product_and_gram(counts, own, sent, near, far, rows_kept, size):
    slots, width = sent.shape[0], own.shape[1]
    in_vmem = pl.BlockSpec(memory_space=pltpu.VMEM)
    anywhere = pl.BlockSpec(memory_space=pl.ANY)
    return pl.pallas_call(
        product_kernel,
        out_shape=(
            jax.ShapeDtypeStruct((rows_kept * size, width), jnp.float32),
            jax.ShapeDtypeStruct((width, width), jnp.float32),
        ),
        in_specs=[pl.BlockSpec(memory_space=pltpu.SMEM)] + [anywhere] * (2 + 2 * PARTS),
        out_specs=(in_vmem, in_vmem),
        scratch_shapes=[
            pltpu.SMEM((slots, SUBLANES, width), jnp.float32),
            pltpu.VMEM((rows_kept, slots, size, size), jnp.float32),
            pltpu.VMEM((rows_kept, slots, size, width), jnp.float32),
            pltpu.SemaphoreType.DMA,
            pltpu.SemaphoreType.DMA((rows_kept,)),
            pltpu.SemaphoreType.DMA((rows_kept, slots)),
        ],
        compiler_params=pltpu.CompilerParams(vmem_limit_bytes=62 << 20),
    )(counts, own, sent, *near, *far)


def factor_kernel(nodes, gram_ref, rows_ref, basis_ref, factor_ref):
    size = gram_ref.shape[0]
    groups = size // SUBLANES
    gram = [gram_ref[SUBLANES * i : SUBLANES * (i + 1), :] for i in range(groups)]
    lane = lax.broadcasted_iota(jnp.int32, (SUBLANES, size), 1)
    sub = lax.broadcasted_iota(jnp.int32, (SUBLANES, size), 0)
    inverse = [(lane == sub + SUBLANES * i).astype(jnp.float32) for i in range(groups)]
    for step in range(size):
        group, within = divmod(step, SUBLANES)
        pivot_row = jnp.broadcast_to(gram[group][within : within + 1, :], (SUBLANES, size))
        inverse_row = jnp.broadcast_to(inverse[group][within : within + 1, :], (SUBLANES, size))
        scale = 1.0 / jnp.broadcast_to(pivot_row[:, step : step + 1], (SUBLANES, size))
        pivot_row, inverse_row = pivot_row * scale, inverse_row * scale
        for other in range(group, groups):
            if other == group and within == SUBLANES - 1:
                continue
            factor = jnp.broadcast_to(gram[other][:, step : step + 1], (SUBLANES, size))
            if other == group:
                factor = jnp.where(sub > within, factor, 0.0)
            gram[other] = gram[other] - factor * pivot_row
            inverse[other] = inverse[other] - factor * inverse_row
    root = jnp.sqrt(jnp.float32(nodes))
    for group in range(groups):
        here = sub + SUBLANES * group
        diagonal = jnp.sum(jnp.where(lane == here, gram[group], 0.0), axis=1, keepdims=True)
        scale = lax.rsqrt(diagonal)
        factor_ref[SUBLANES * group : SUBLANES * (group + 1), :] = jnp.where(lane >= here, gram[group] * scale, 0.0) / root
        inverse[group] = inverse[group] * (scale * root)
    basis_ref[...] = lax.dot_general(
        rows_ref[...], jnp.concatenate(inverse, axis=0), (((1,), (1,)), ((), ())),
        precision=EXACT, preferred_element_type=jnp.float32,
    )


def basis_and_factor(nodes, gram, rows):
    in_vmem = pl.BlockSpec(memory_space=pltpu.VMEM)
    return pl.pallas_call(
        functools.partial(factor_kernel, nodes),
        out_shape=(jax.ShapeDtypeStruct(rows.shape, jnp.float32), jax.ShapeDtypeStruct(gram.shape, jnp.float32)),
        in_specs=[in_vmem] * 2,
        out_specs=(in_vmem, in_vmem),
        compiler_params=pltpu.CompilerParams(vmem_limit_bytes=62 << 20),
    )(gram, rows)


def device_groups(row_devices, col_devices, row_step, key):
    groups = {}
    for row, col in itertools.product(range(row_devices), range(col_devices)):
        groups.setdefault(key(row // row_step, row % row_step, col), []).append(row * col_devices + col)
    return list(groups.values())


def exchange(pieces, groups):
    return lax.all_to_all(pieces, ("rows", "cols"), 0, 0, axis_index_groups=groups, tiled=True)


def sum_over_devices(gram, row_devices, col_devices):
    row_step = 4
    plane = device_groups(row_devices, col_devices, row_step, lambda z, y, col: z)
    across = device_groups(row_devices, col_devices, row_step, lambda z, y, col: (y, col))
    in_plane, planes = len(plane[0]), len(across[0])
    size, width = gram.shape
    piece = exchange(gram.reshape(in_plane, size // in_plane, width), plane).sum(0)
    piece = exchange(jnp.broadcast_to(piece[None], (planes,) + piece.shape), across).sum(0)
    return exchange(jnp.broadcast_to(piece[None], (in_plane,) + piece.shape), plane).reshape(size, width)


def on_device(block_vector, op_tiles, tile_cols, live_counts):
    block_count, _, size, width = op_tiles.shape
    row_devices, col_devices = lax.axis_size("rows"), lax.axis_size("cols")
    row = lax.axis_index("rows")
    rows_here = block_count * size
    rows_kept = block_count // col_devices

    def fetched_by(r, c):
        if c % 2 == 0:
            return (r, c + 1) if r == row_devices - 1 else (r + 1, c)
        return (r, c - 1) if r == 0 else (r - 1, c)

    steps = []
    for r, c in itertools.product(range(row_devices), range(col_devices)):
        to_r, to_c = fetched_by(r, c)
        steps.append((r * col_devices + c, to_r * col_devices + to_c))
    rows_part = rows_here // PARTS
    near = []
    for at in range(PARTS):
        source = lax.optimization_barrier(block_vector) if at else block_vector
        near.append(lax.ppermute(source[at * rows_part : (at + 1) * rows_part], ("rows", "cols"), steps))
    far = [lax.ppermute(part, "cols", [(i, i ^ 1) for i in range(col_devices)]) for part in near]

    numbers = (tile_cols - (row - 1) * block_count).reshape(col_devices, rows_kept)
    places = jnp.arange(col_devices, dtype=jnp.int32)[:, None]
    note = jnp.concatenate([numbers, places], axis=1).astype(jnp.float32)
    note = jnp.pad(note[:, None, :], ((0, 0), (0, SUBLANES - 1), (0, size - rows_kept - 1)))
    sent = jnp.concatenate([op_tiles.reshape(col_devices, rows_kept * size, size), note], axis=1)
    sent = lax.all_to_all(sent, "cols", 0, 0, tiled=True)
    part_rows, gram = product_and_gram(live_counts, block_vector, sent, near, far, rows_kept, size)
    gram = sum_over_devices(gram, row_devices, col_devices)
    return basis_and_factor(rows_here * row_devices, gram, part_rows)


def solution(mesh):
    in_specs = (P("rows", None), P("rows", "cols", None, None), P("rows", "cols"), P("rows"))
    out_specs = (P(("rows", "cols"), None), P())
    return jax.shard_map(
        on_device, mesh=mesh, in_specs=in_specs, out_specs=out_specs, check_vma=False
    )
```

```python
import functools
import itertools

import jax
import jax.numpy as jnp
from jax import lax
from jax.experimental import pallas as pl
from jax.experimental.pallas import tpu as pltpu
from jax.sharding import PartitionSpec as P

EXACT = lax.Precision.HIGHEST
SUBLANES = 8
PARTS = 2


def split_bf16(x):
    high = x.astype(jnp.bfloat16)
    low = (x - high.astype(jnp.float32)).astype(jnp.bfloat16)
    return high, low


def product_kernel(
    count_ref, own_ref, sent_ref, *refs,
):
    near_ref, far_refs = refs[0], refs[1 : 1 + PARTS]
    out_ref, gram_ref, note_buf, tile_buf, vec_buf, note_sem, tile_sem, vec_sem = refs[1 + PARTS :]
    slots = sent_ref.shape[0]
    size, width = tile_buf.shape[2:]
    rows_kept = out_ref.shape[0] // size
    blocks = own_ref.shape[0] // size
    part = blocks // PARTS

    def copy_tiles(row):
        start = pl.multiple_of(row * size, size)
        return pltpu.make_async_copy(sent_ref.at[:, pl.ds(start, size)], tile_buf.at[row], tile_sem.at[row])

    def copy_vec(source, block, row, slot):
        start = pl.multiple_of(block * size, size)
        return pltpu.make_async_copy(source.at[pl.ds(start, size)], vec_buf.at[row, slot], vec_sem.at[row, slot])

    notes = pltpu.make_async_copy(sent_ref.at[:, pl.ds(rows_kept * size, SUBLANES)], note_buf, note_sem)
    notes.start()
    copy_tiles(0).start()
    notes.wait()
    col = note_buf[0, 0, rows_kept].astype(jnp.int32)
    first_row, near_side = col * rows_kept, 2 * (col % 2)

    def fetch(row, carry):
        @pl.when(row > 0)
        def _():
            copy_tiles(row).start()

        def fetch_vec(slot, inner):
            block = note_buf[slot, 0, row].astype(jnp.int32)
            side, within = block // blocks, block % blocks

            @pl.when(side == 1)
            def _():
                copy_vec(own_ref, within, row, slot).start()

            @pl.when(side == near_side)
            def _():
                copy_vec(near_ref, within, row, slot).start()

            for at in range(PARTS):

                @pl.when((side != 1) & (side != near_side) & (within // part == at))
                def _():
                    copy_vec(far_refs[at], within % part, row, slot).start()

            return inner

        return lax.fori_loop(0, count_ref[first_row + row], fetch_vec, carry)

    lax.fori_loop(0, rows_kept, fetch, 0)

    def row_block(row, carry):
        count = count_ref[first_row + row]
        copy_tiles(row).wait()

        def wait_vec(slot, inner):
            copy_vec(own_ref, 0, row, slot).wait()
            return inner

        lax.fori_loop(0, count, wait_vec, 0)
        total = jnp.zeros((size, width), jnp.float32)
        for slot in range(0, slots, 2):
            pair = (slot, slot + 1)
            tiles = [tile_buf[row, one] for one in pair]
            vecs = [jnp.where(one < count, vec_buf[row, one], 0.0) for one in pair]
            tile_high, tile_low = split_bf16(jnp.concatenate(tiles, axis=1))
            vec_high, vec_low = split_bf16(jnp.concatenate(vecs, axis=0))
            both = jnp.dot(
                tile_high, jnp.concatenate([vec_high, vec_low], axis=1), preferred_element_type=jnp.float32
            )
            total += both[:, :width] + both[:, width:]
            total += jnp.dot(tile_low, vec_high, preferred_element_type=jnp.float32)
        out_ref[pl.ds(pl.multiple_of(row * size, size), size), :] = total
        return carry

    lax.fori_loop(0, rows_kept, row_block, 0)
    high, low = split_bf16(out_ref[...])
    both = jnp.concatenate([high, low], axis=1)
    gram = lax.dot_general(both, both, (((0,), (0,)), ((), ())), preferred_element_type=jnp.float32)
    gram_ref[...] = gram[:width, :width] + (gram[:width, width:] + gram[width:, :width]) + gram[width:, width:]


def product_and_gram(counts, own, sent, near, far, rows_kept, size):
    slots, width = sent.shape[0], own.shape[1]
    in_vmem = pl.BlockSpec(memory_space=pltpu.VMEM)
    anywhere = pl.BlockSpec(memory_space=pl.ANY)
    return pl.pallas_call(
        product_kernel,
        out_shape=(
            jax.ShapeDtypeStruct((rows_kept * size, width), jnp.float32),
            jax.ShapeDtypeStruct((width, width), jnp.float32),
        ),
        in_specs=[pl.BlockSpec(memory_space=pltpu.SMEM)] + [anywhere] * (3 + PARTS),
        out_specs=(in_vmem, in_vmem),
        scratch_shapes=[
            pltpu.SMEM((slots, SUBLANES, width), jnp.float32),
            pltpu.VMEM((rows_kept, slots, size, size), jnp.float32),
            pltpu.VMEM((rows_kept, slots, size, width), jnp.float32),
            pltpu.SemaphoreType.DMA,
            pltpu.SemaphoreType.DMA((rows_kept,)),
            pltpu.SemaphoreType.DMA((rows_kept, slots)),
        ],
        compiler_params=pltpu.CompilerParams(vmem_limit_bytes=62 << 20),
    )(counts, own, sent, near, *far)


def factor_kernel(nodes, gram_ref, rows_ref, basis_ref, factor_ref):
    size = gram_ref.shape[0]
    groups = size // SUBLANES
    shape = (SUBLANES, size)
    lane = lax.broadcasted_iota(jnp.int32, shape, 1)
    sub = lax.broadcasted_iota(jnp.int32, shape, 0)
    root = jnp.sqrt(jnp.float32(nodes))

    def column(x, at):
        return jnp.broadcast_to(x[:, at : at + 1], shape)

    def line(x, at):
        return jnp.broadcast_to(x[at : at + 1, :], shape)

    def total(terms):
        while len(terms) > 1:
            terms = [terms[i] + terms[i + 1] for i in range(0, len(terms), 2)]
        return terms[0]

    gram = [gram_ref[SUBLANES * i : SUBLANES * (i + 1), :] for i in range(groups)]
    inverse = [(lane == sub + SUBLANES * i).astype(jnp.float32) for i in range(groups)]
    for group in range(groups):
        first = SUBLANES * group
        x, v = gram[group], inverse[group]
        columns = [column(x, first + i) for i in range(SUBLANES)]
        upper, solved, pivots = jnp.zeros(shape), jnp.zeros(shape), jnp.ones(shape)
        for i in range(SUBLANES):
            here = sub == i
            pivot = line(columns[i], i)
            scale = 1.0 / pivot
            x_line, v_line = line(x, i), line(v, i)
            upper, solved = jnp.where(here, x_line, upper), jnp.where(here, v_line, solved)
            pivots = jnp.where(here, pivot, pivots)
            weight = columns[i] * scale
            x = jnp.where(here, x_line * scale, x - weight * x_line)
            v = jnp.where(here, v_line * scale, v - weight * v_line)
            for j in range(i + 1, SUBLANES):
                c_line = line(columns[j], i)
                columns[j] = jnp.where(here, c_line * scale, columns[j] - weight * c_line)
        norm = lax.rsqrt(pivots)
        factor_ref[first : first + SUBLANES, :] = jnp.where(lane >= sub + first, upper * norm, 0.0) / root
        inverse[group] = solved * (norm * root)
        x_lines, v_lines = [line(x, i) for i in range(SUBLANES)], [line(v, i) for i in range(SUBLANES)]
        for below in range(group + 1, groups):
            weights = [column(gram[below], first + i) for i in range(SUBLANES)]
            gram[below] = gram[below] - total([weights[i] * x_lines[i] for i in range(SUBLANES)])
            inverse[below] = inverse[below] - total([weights[i] * v_lines[i] for i in range(SUBLANES)])
    basis_ref[...] = lax.dot_general(
        rows_ref[...], jnp.concatenate(inverse, axis=0), (((1,), (1,)), ((), ())),
        precision=EXACT, preferred_element_type=jnp.float32,
    )


def basis_and_factor(nodes, gram, rows):
    in_vmem = pl.BlockSpec(memory_space=pltpu.VMEM)
    return pl.pallas_call(
        functools.partial(factor_kernel, nodes),
        out_shape=(jax.ShapeDtypeStruct(rows.shape, jnp.float32), jax.ShapeDtypeStruct(gram.shape, jnp.float32)),
        in_specs=[in_vmem] * 2,
        out_specs=(in_vmem, in_vmem),
        compiler_params=pltpu.CompilerParams(vmem_limit_bytes=62 << 20),
    )(gram, rows)


def device_groups(row_devices, col_devices, row_step, key):
    groups = {}
    for row, col in itertools.product(range(row_devices), range(col_devices)):
        groups.setdefault(key(row // row_step, row % row_step, col), []).append(row * col_devices + col)
    return list(groups.values())


def exchange(pieces, groups):
    return lax.all_to_all(pieces, ("rows", "cols"), 0, 0, axis_index_groups=groups, tiled=True)


def sum_over_devices(gram, row_devices, col_devices):
    row_step = 4
    plane = device_groups(row_devices, col_devices, row_step, lambda z, y, col: z)
    across = device_groups(row_devices, col_devices, row_step, lambda z, y, col: (y, col))
    in_plane, planes = len(plane[0]), len(across[0])
    size, width = gram.shape
    piece = exchange(gram.reshape(in_plane, size // in_plane, width), plane).sum(0)
    piece = exchange(jnp.broadcast_to(piece[None], (planes,) + piece.shape), across).sum(0)
    return exchange(jnp.broadcast_to(piece[None], (in_plane,) + piece.shape), plane).reshape(size, width)


def on_device(block_vector, op_tiles, tile_cols, live_counts):
    block_count, _, size, width = op_tiles.shape
    row_devices, col_devices = lax.axis_size("rows"), lax.axis_size("cols")
    row = lax.axis_index("rows")
    rows_here = block_count * size
    rows_kept = block_count // col_devices

    def fetched_by(r, c):
        if c % 2 == 0:
            return (r, c + 1) if r == row_devices - 1 else (r + 1, c)
        return (r, c - 1) if r == 0 else (r - 1, c)

    steps = []
    for r, c in itertools.product(range(row_devices), range(col_devices)):
        to_r, to_c = fetched_by(r, c)
        steps.append((r * col_devices + c, to_r * col_devices + to_c))
    rows_part = rows_here // PARTS
    near = lax.ppermute(block_vector, ("rows", "cols"), steps)
    far = []
    for at in range(PARTS):
        source = lax.optimization_barrier(near) if at else near
        part = source[at * rows_part : (at + 1) * rows_part]
        far.append(lax.ppermute(part, "cols", [(i, i ^ 1) for i in range(col_devices)]))

    numbers = (tile_cols - (row - 1) * block_count).reshape(col_devices, rows_kept)
    places = jnp.arange(col_devices, dtype=jnp.int32)[:, None]
    note = jnp.concatenate([numbers, places], axis=1).astype(jnp.float32)
    note = jnp.pad(note[:, None, :], ((0, 0), (0, SUBLANES - 1), (0, size - rows_kept - 1)))
    sent = jnp.concatenate([op_tiles.reshape(col_devices, rows_kept * size, size), note], axis=1)
    sent = lax.all_to_all(sent, "cols", 0, 0, tiled=True)
    part_rows, gram = product_and_gram(live_counts, block_vector, sent, near, far, rows_kept, size)
    gram = sum_over_devices(gram, row_devices, col_devices)
    return basis_and_factor(rows_here * row_devices, gram, part_rows)


def solution(mesh):
    in_specs = (P("rows", None), P("rows", "cols", None, None), P("rows", "cols"), P("rows"))
    out_specs = (P(("rows", "cols"), None), P())
    return jax.shard_map(
        on_device, mesh=mesh, in_specs=in_specs, out_specs=out_specs, check_vma=False
    )
```

```python
import functools
import itertools

import jax
import jax.numpy as jnp
from jax import lax
from jax.experimental import pallas as pl
from jax.experimental.pallas import tpu as pltpu
from jax.sharding import PartitionSpec as P

EXACT = lax.Precision.HIGHEST
SUBLANES = 8
PANEL = 2
CHUNKS = 4
PARTS = 2


def split_bf16(x):
    high = x.astype(jnp.bfloat16)
    low = (x - high.astype(jnp.float32)).astype(jnp.bfloat16)
    return high, low


def product_kernel(own_ref, sent_ref, *refs):
    near_ref, far_refs = refs[0], refs[1 : 1 + PARTS]
    out_ref, gram_ref, note_buf, tile_buf, vec_buf, note_sem, tile_sem, vec_sem = refs[1 + PARTS :]
    slots = sent_ref.shape[0]
    size, width = tile_buf.shape[2:]
    rows_kept = out_ref.shape[0] // size
    blocks = own_ref.shape[0] // size
    part = blocks // PARTS

    def copy_tiles(row):
        start = pl.multiple_of(row * size, size)
        return pltpu.make_async_copy(sent_ref.at[:, pl.ds(start, size)], tile_buf.at[row], tile_sem.at[row])

    def copy_vec(source, block, row, slot):
        start = pl.multiple_of(block * size, size)
        return pltpu.make_async_copy(source.at[pl.ds(start, size)], vec_buf.at[row, slot], vec_sem.at[row, slot])

    notes = pltpu.make_async_copy(sent_ref.at[:, pl.ds(rows_kept * size, 1)], note_buf, note_sem)
    notes.start()
    copy_tiles(0).start()
    notes.wait()
    col = note_buf[0, 0, rows_kept].astype(jnp.int32)
    near_side = 2 * (col % 2)

    def count_of(row):
        return note_buf[0, 0, rows_kept + 1 + row].astype(jnp.int32)

    def fetch(row, carry):
        @pl.when(row > 0)
        def _():
            copy_tiles(row).start()

        def fetch_vec(slot, inner):
            block = note_buf[slot, 0, row].astype(jnp.int32)
            side = (block >= blocks).astype(jnp.int32) + (block >= 2 * blocks).astype(jnp.int32)
            within = block - side * blocks

            @pl.when(side == 1)
            def _():
                copy_vec(own_ref, within, row, slot).start()

            @pl.when(side == near_side)
            def _():
                copy_vec(near_ref, within, row, slot).start()

            @pl.when(side == 2 - near_side)
            def _():
                for at in range(PARTS):

                    @pl.when((within >= at * part) & (within < (at + 1) * part))
                    def _():
                        copy_vec(far_refs[at], within - at * part, row, slot).start()

            return inner

        return lax.fori_loop(0, count_of(row), fetch_vec, carry)

    lax.fori_loop(0, rows_kept, fetch, 0)

    def row_block(row, carry):
        count = count_of(row)
        copy_tiles(row).wait()

        def wait_vec(slot, inner):
            copy_vec(own_ref, 0, row, slot).wait()
            return inner

        lax.fori_loop(0, count, wait_vec, 0)
        total = jnp.zeros((size, width), jnp.float32)
        for slot in range(0, slots, 2):
            pair = (slot, slot + 1)
            tiles = [tile_buf[row, one] for one in pair]
            vecs = [jnp.where(one < count, vec_buf[row, one], 0.0) for one in pair]
            tile_high, tile_low = split_bf16(jnp.concatenate(tiles, axis=1))
            vec_high, vec_low = split_bf16(jnp.concatenate(vecs, axis=0))
            both = jnp.dot(
                tile_high, jnp.concatenate([vec_high, vec_low], axis=1), preferred_element_type=jnp.float32
            )
            total += both[:, :width] + both[:, width:]
            total += jnp.dot(tile_low, vec_high, preferred_element_type=jnp.float32)
        out_ref[pl.ds(pl.multiple_of(row * size, size), size), :] = total
        return carry

    lax.fori_loop(0, rows_kept, row_block, 0)
    high, low = split_bf16(out_ref[...])
    both = jnp.concatenate([high, low], axis=1)
    gram = lax.dot_general(both, both, (((0,), (0,)), ((), ())), preferred_element_type=jnp.float32)
    gram_ref[...] = gram[:width, :width] + (gram[:width, width:] + gram[width:, :width]) + gram[width:, width:]


def product_and_gram(own, sent, near, far, rows_kept, size):
    slots, width = sent.shape[0], own.shape[1]
    in_vmem = pl.BlockSpec(memory_space=pltpu.VMEM)
    anywhere = pl.BlockSpec(memory_space=pl.ANY)
    return pl.pallas_call(
        product_kernel,
        out_shape=(
            jax.ShapeDtypeStruct((rows_kept * size, width), jnp.float32),
            jax.ShapeDtypeStruct((width, width), jnp.float32),
        ),
        in_specs=[anywhere] * (3 + PARTS),
        out_specs=(in_vmem, in_vmem),
        scratch_shapes=[
            pltpu.SMEM((slots, 1, width), jnp.float32),
            pltpu.VMEM((rows_kept, slots, size, size), jnp.float32),
            pltpu.VMEM((rows_kept, slots, size, width), jnp.float32),
            pltpu.SemaphoreType.DMA,
            pltpu.SemaphoreType.DMA((rows_kept,)),
            pltpu.SemaphoreType.DMA((rows_kept, slots)),
        ],
        compiler_params=pltpu.CompilerParams(vmem_limit_bytes=62 << 20),
    )(own, sent, near, *far)


def factor_kernel(nodes, gram_ref, rows_ref, basis_ref, factor_ref, rows_buf, basis_buf, rows_sem, basis_sem):
    size = gram_ref.shape[0]
    groups = size // SUBLANES
    shape = (SUBLANES, size)
    lane = lax.broadcasted_iota(jnp.int32, shape, 1)
    sub = lax.broadcasted_iota(jnp.int32, shape, 0)
    root = jnp.sqrt(jnp.float32(nodes))
    bring = pltpu.make_async_copy(rows_ref, rows_buf, rows_sem)
    bring.start()

    def column(x, at):
        return jnp.broadcast_to(x[:, at : at + 1], shape)

    def line(x, at):
        return jnp.broadcast_to(x[at : at + 1, :], shape)

    def total(terms):
        while len(terms) > 1:
            terms = [terms[i] + terms[i + 1] for i in range(0, len(terms), 2)]
        return terms[0]

    gram = [gram_ref[SUBLANES * i : SUBLANES * (i + 1), :] for i in range(groups)]
    inverse = [(lane == sub + SUBLANES * i).astype(jnp.float32) for i in range(groups)]
    for start in range(0, groups, PANEL):
        first = SUBLANES * start
        height = SUBLANES * PANEL
        rows = range(PANEL)
        x, v = gram[start : start + PANEL], inverse[start : start + PANEL]
        columns = [[column(x[q], first + i) for q in rows] for i in range(height)]
        upper, solved, pivots = list(x), list(v), [jnp.ones(shape) for q in rows]
        for i in range(height):
            at, within = divmod(i, SUBLANES)
            here = sub == within
            pivot = line(columns[i][at], within)
            x_line, v_line = line(x[at], within), line(v[at], within)
            upper[at], solved[at] = jnp.where(here, x_line, upper[at]), jnp.where(here, v_line, solved[at])
            pivots[at] = jnp.where(here, pivot, pivots[at])
            scale = 1.0 / pivot
            weight = [columns[i][q] * scale for q in rows]
            weight[at] = jnp.where(here, 0.0, weight[at])
            for q in rows:
                x[q], v[q] = x[q] - weight[q] * x_line, v[q] - weight[q] * v_line
            for j in range(i + 1, height):
                c_line = line(columns[j][at], within)
                for q in rows:
                    columns[j][q] = columns[j][q] - weight[q] * c_line
        x_lines, v_lines = [], []
        for q in rows:
            scale, norm, begin = 1.0 / pivots[q], lax.rsqrt(pivots[q]), first + SUBLANES * q
            factor_ref[begin : begin + SUBLANES, :] = jnp.where(lane >= sub + begin, upper[q] * norm, 0.0) / root
            inverse[start + q] = solved[q] * (norm * root)
            x[q], v[q] = x[q] * scale, v[q] * scale
            x_lines += [line(x[q], i) for i in range(SUBLANES)]
            v_lines += [line(v[q], i) for i in range(SUBLANES)]
        for below in range(start + PANEL, groups):
            weights = [column(gram[below], first + i) for i in range(height)]
            gram[below] = gram[below] - total([weights[i] * x_lines[i] for i in range(height)])
            inverse[below] = inverse[below] - total([weights[i] * v_lines[i] for i in range(height)])
    solver = jnp.concatenate(inverse, axis=0)
    bring.wait()
    chunk = rows_buf.shape[0] // CHUNKS
    copies = []
    for at in range(CHUNKS):
        here = pl.ds(at * chunk, chunk)
        basis_buf[here, :] = lax.dot_general(
            rows_buf[here, :], solver, (((1,), (1,)), ((), ())), precision=EXACT, preferred_element_type=jnp.float32
        )
        copies.append(pltpu.make_async_copy(basis_buf.at[here], basis_ref.at[here], basis_sem.at[at]))
        copies[-1].start()
    for copy in copies:
        copy.wait()


def basis_and_factor(nodes, gram, rows):
    in_vmem = pl.BlockSpec(memory_space=pltpu.VMEM)
    in_hbm = pl.BlockSpec(memory_space=pltpu.HBM)
    return pl.pallas_call(
        functools.partial(factor_kernel, nodes),
        out_shape=(jax.ShapeDtypeStruct(rows.shape, jnp.float32), jax.ShapeDtypeStruct(gram.shape, jnp.float32)),
        in_specs=[in_vmem, in_hbm],
        out_specs=(in_hbm, in_vmem),
        scratch_shapes=[
            pltpu.VMEM(rows.shape, jnp.float32),
            pltpu.VMEM(rows.shape, jnp.float32),
            pltpu.SemaphoreType.DMA,
            pltpu.SemaphoreType.DMA((CHUNKS,)),
        ],
        compiler_params=pltpu.CompilerParams(vmem_limit_bytes=62 << 20),
    )(gram, rows)


def device_groups(row_devices, col_devices, row_step, key):
    groups = {}
    for row, col in itertools.product(range(row_devices), range(col_devices)):
        groups.setdefault(key(row // row_step, row % row_step, col), []).append(row * col_devices + col)
    return list(groups.values())


def exchange(pieces, groups):
    return lax.all_to_all(pieces, ("rows", "cols"), 0, 0, axis_index_groups=groups, tiled=True)


def sum_over_devices(gram, row_devices, col_devices):
    row_step = 4
    plane = device_groups(row_devices, col_devices, row_step, lambda z, y, col: z)
    across = device_groups(row_devices, col_devices, row_step, lambda z, y, col: (y, col))
    in_plane, planes = len(plane[0]), len(across[0])
    size, width = gram.shape
    piece = exchange(gram.reshape(in_plane, size // in_plane, width), plane).sum(0)
    piece = exchange(jnp.broadcast_to(piece[None], (planes,) + piece.shape), across).sum(0)
    return exchange(jnp.broadcast_to(piece[None], (in_plane,) + piece.shape), plane).reshape(size, width)


def on_device(block_vector, op_tiles, tile_cols, live_counts):
    block_count, _, size, width = op_tiles.shape
    row_devices, col_devices = lax.axis_size("rows"), lax.axis_size("cols")
    row = lax.axis_index("rows")
    rows_here = block_count * size
    rows_kept = block_count // col_devices

    def fetched_by(r, c):
        if c % 2 == 0:
            return (r, c + 1) if r == row_devices - 1 else (r + 1, c)
        return (r, c - 1) if r == 0 else (r - 1, c)

    steps = []
    for r, c in itertools.product(range(row_devices), range(col_devices)):
        to_r, to_c = fetched_by(r, c)
        steps.append((r * col_devices + c, to_r * col_devices + to_c))
    rows_part = rows_here // PARTS
    near = lax.ppermute(block_vector, ("rows", "cols"), steps)
    far = []
    for at in range(PARTS):
        source = lax.optimization_barrier(near) if at else near
        part = source[at * rows_part : (at + 1) * rows_part]
        far.append(lax.ppermute(part, "cols", [(i, i ^ 1) for i in range(col_devices)]))

    numbers = (tile_cols - (row - 1) * block_count).reshape(col_devices, rows_kept)
    places = jnp.arange(col_devices, dtype=jnp.int32)[:, None]
    counts = live_counts.reshape(col_devices, rows_kept)
    note = jnp.concatenate([numbers, places, counts], axis=1).astype(jnp.float32)
    note = jnp.pad(note[:, None, :], ((0, 0), (0, SUBLANES - 1), (0, size - note.shape[1])))
    sent = jnp.concatenate([op_tiles.reshape(col_devices, rows_kept * size, size), note], axis=1)
    sent = lax.all_to_all(sent, "cols", 0, 0, tiled=True)
    part_rows, gram = product_and_gram(block_vector, sent, near, far, rows_kept, size)
    gram = sum_over_devices(gram, row_devices, col_devices)
    return basis_and_factor(rows_here * row_devices, gram, part_rows)


def solution(mesh):
    in_specs = (P("rows", None), P("rows", "cols", None, None), P("rows", "cols"), P("rows"))
    out_specs = (P(("rows", "cols"), None), P())
    return jax.shard_map(
        on_device, mesh=mesh, in_specs=in_specs, out_specs=out_specs, check_vma=False
    )
```

```python
import functools
import itertools

import jax
import jax.numpy as jnp
from jax import lax
from jax.experimental import pallas as pl
from jax.experimental.pallas import tpu as pltpu
from jax.sharding import PartitionSpec as P

EXACT = lax.Precision.HIGHEST
SUBLANES = 8
PANEL = 2
CHUNKS = 4


def split_bf16(x):
    high = x.astype(jnp.bfloat16)
    low = (x - high.astype(jnp.float32)).astype(jnp.bfloat16)
    return high, low


def product_kernel(
    table_ref, own_ref, sent_ref, near_ref, far_ref, out_ref, gram_ref, tile_buf, vec_buf, tile_sem, vec_sem
):
    slots = sent_ref.shape[0]
    size, width = tile_buf.shape[2:]
    rows_kept = out_ref.shape[0] // size
    blocks = own_ref.shape[0] // size

    def copy_tiles(row):
        start = pl.multiple_of(row * size, size)
        return pltpu.make_async_copy(sent_ref.at[:, pl.ds(start, size)], tile_buf.at[row], tile_sem.at[row])

    def copy_vec(source, block, row, slot):
        start = pl.multiple_of(block * size, size)
        return pltpu.make_async_copy(source.at[pl.ds(start, size)], vec_buf.at[row, slot], vec_sem.at[row, slot])

    copy_tiles(0).start()
    kept_from, near_side = table_ref[slots + 1, 0] * rows_kept, table_ref[slots + 1, 1]

    def count_of(row):
        return table_ref[slots, kept_from + row]

    def fetch(row, carry):
        @pl.when(row > 0)
        def _():
            copy_tiles(row).start()

        def fetch_vec(slot, inner):
            block = table_ref[slot, kept_from + row]
            side = (block >= blocks).astype(jnp.int32) + (block >= 2 * blocks).astype(jnp.int32)
            within = block - side * blocks

            @pl.when(side == 1)
            def _():
                copy_vec(own_ref, within, row, slot).start()

            @pl.when(side == near_side)
            def _():
                copy_vec(near_ref, within, row, slot).start()

            @pl.when(side == 2 - near_side)
            def _():
                copy_vec(far_ref, within, row, slot).start()

            return inner

        return lax.fori_loop(0, count_of(row), fetch_vec, carry)

    lax.fori_loop(0, rows_kept, fetch, 0)

    def row_block(row, carry):
        count = count_of(row)
        copy_tiles(row).wait()

        def wait_vec(slot, inner):
            copy_vec(own_ref, 0, row, slot).wait()
            return inner

        lax.fori_loop(0, count, wait_vec, 0)
        total = jnp.zeros((size, width), jnp.float32)
        for slot in range(0, slots, 2):
            pair = (slot, slot + 1)
            tiles = [tile_buf[row, one] for one in pair]
            vecs = [jnp.where(one < count, vec_buf[row, one], 0.0) for one in pair]
            tile_high, tile_low = split_bf16(jnp.concatenate(tiles, axis=1))
            vec_high, vec_low = split_bf16(jnp.concatenate(vecs, axis=0))
            both = jnp.dot(
                tile_high, jnp.concatenate([vec_high, vec_low], axis=1), preferred_element_type=jnp.float32
            )
            total += both[:, :width] + both[:, width:]
            total += jnp.dot(tile_low, vec_high, preferred_element_type=jnp.float32)
        out_ref[pl.ds(pl.multiple_of(row * size, size), size), :] = total
        return carry

    lax.fori_loop(0, rows_kept, row_block, 0)
    high, low = split_bf16(out_ref[...])
    both = jnp.concatenate([high, low], axis=1)
    gram = lax.dot_general(both, both, (((0,), (0,)), ((), ())), preferred_element_type=jnp.float32)
    gram_ref[...] = gram[:width, :width] + (gram[:width, width:] + gram[width:, :width]) + gram[width:, width:]


def decode_kernel(first, count_ref, sent_ref, table_ref, note_buf, sem):
    notes = pltpu.make_async_copy(sent_ref.at[:, pl.ds(first, SUBLANES)], note_buf, sem)
    notes.start()
    slots = note_buf.shape[0]
    blocks = count_ref.shape[1]
    row, col = lax.axis_index("rows"), lax.axis_index("cols")
    table_ref[slots : slots + 1, :blocks] = count_ref[...]
    at = lax.broadcasted_iota(jnp.int32, (1, table_ref.shape[1]), 1)
    table_ref[slots + 1 : slots + 2, :] = jnp.where(at == 0, col, 2 * (col % 2))
    notes.wait()
    for slot in range(slots):
        table_ref[slot : slot + 1, :] = note_buf[slot, 0:1, :].astype(jnp.int32) - (row - 1) * blocks


def decode(counts, sent, first):
    slots, _, size = sent.shape
    return pl.pallas_call(
        functools.partial(decode_kernel, first),
        out_shape=jax.ShapeDtypeStruct((slots + SUBLANES, size), jnp.int32),
        in_specs=[pl.BlockSpec(memory_space=pltpu.VMEM), pl.BlockSpec(memory_space=pl.ANY)],
        out_specs=pl.BlockSpec(memory_space=pltpu.VMEM),
        scratch_shapes=[pltpu.VMEM((slots, SUBLANES, size), jnp.float32), pltpu.SemaphoreType.DMA],
        compiler_params=pltpu.CompilerParams(vmem_limit_bytes=62 << 20),
        cost_estimate=pl.CostEstimate(flops=1 << 33, bytes_accessed=1 << 26, transcendentals=0),
    )(counts, sent)


def product_and_gram(table, own, sent, near, far, rows_kept, size):
    slots, width = sent.shape[0], own.shape[1]
    in_vmem = pl.BlockSpec(memory_space=pltpu.VMEM)
    anywhere = pl.BlockSpec(memory_space=pl.ANY)
    return pl.pallas_call(
        product_kernel,
        out_shape=(
            jax.ShapeDtypeStruct((rows_kept * size, width), jnp.float32),
            jax.ShapeDtypeStruct((width, width), jnp.float32),
        ),
        in_specs=[pl.BlockSpec(memory_space=pltpu.SMEM)] + [anywhere] * 4,
        out_specs=(in_vmem, in_vmem),
        scratch_shapes=[
            pltpu.VMEM((rows_kept, slots, size, size), jnp.float32),
            pltpu.VMEM((rows_kept, slots, size, width), jnp.float32),
            pltpu.SemaphoreType.DMA((rows_kept,)),
            pltpu.SemaphoreType.DMA((rows_kept, slots)),
        ],
        compiler_params=pltpu.CompilerParams(vmem_limit_bytes=62 << 20),
    )(table, own, sent, near, far)


def factor_kernel(nodes, gram_ref, rows_ref, basis_ref, factor_ref, rows_buf, basis_buf, rows_sem, basis_sem):
    size = gram_ref.shape[0]
    groups = size // SUBLANES
    shape = (SUBLANES, size)
    lane = lax.broadcasted_iota(jnp.int32, shape, 1)
    sub = lax.broadcasted_iota(jnp.int32, shape, 0)
    root = jnp.sqrt(jnp.float32(nodes))
    bring = pltpu.make_async_copy(rows_ref, rows_buf, rows_sem)
    bring.start()

    def column(x, at):
        return jnp.broadcast_to(x[:, at : at + 1], shape)

    def line(x, at):
        return jnp.broadcast_to(x[at : at + 1, :], shape)

    def total(terms):
        while len(terms) > 1:
            terms = [terms[i] + terms[i + 1] for i in range(0, len(terms), 2)]
        return terms[0]

    gram = [gram_ref[SUBLANES * i : SUBLANES * (i + 1), :] for i in range(groups)]
    inverse = [(lane == sub + SUBLANES * i).astype(jnp.float32) for i in range(groups)]
    for start in range(0, groups, PANEL):
        first = SUBLANES * start
        height = SUBLANES * PANEL
        rows = range(PANEL)
        x, v = gram[start : start + PANEL], inverse[start : start + PANEL]
        columns = [[column(x[q], first + i) for q in rows] for i in range(height)]
        upper, solved, pivots = list(x), list(v), [jnp.ones(shape) for q in rows]
        for i in range(height):
            at, within = divmod(i, SUBLANES)
            here = sub == within
            pivot = line(columns[i][at], within)
            x_line, v_line = line(x[at], within), line(v[at], within)
            upper[at], solved[at] = jnp.where(here, x_line, upper[at]), jnp.where(here, v_line, solved[at])
            pivots[at] = jnp.where(here, pivot, pivots[at])
            scale = 1.0 / pivot
            weight = [columns[i][q] * scale for q in rows]
            weight[at] = jnp.where(here, 0.0, weight[at])
            for q in rows:
                x[q], v[q] = x[q] - weight[q] * x_line, v[q] - weight[q] * v_line
            for j in range(i + 1, height):
                c_line = line(columns[j][at], within)
                for q in rows:
                    columns[j][q] = columns[j][q] - weight[q] * c_line
        x_lines, v_lines = [], []
        for q in rows:
            scale, norm, begin = 1.0 / pivots[q], lax.rsqrt(pivots[q]), first + SUBLANES * q
            factor_ref[begin : begin + SUBLANES, :] = jnp.where(lane >= sub + begin, upper[q] * norm, 0.0) / root
            inverse[start + q] = solved[q] * (norm * root)
            x[q], v[q] = x[q] * scale, v[q] * scale
            x_lines += [line(x[q], i) for i in range(SUBLANES)]
            v_lines += [line(v[q], i) for i in range(SUBLANES)]
        for below in range(start + PANEL, groups):
            weights = [column(gram[below], first + i) for i in range(height)]
            gram[below] = gram[below] - total([weights[i] * x_lines[i] for i in range(height)])
            inverse[below] = inverse[below] - total([weights[i] * v_lines[i] for i in range(height)])
    solver = jnp.concatenate(inverse, axis=0)
    bring.wait()
    chunk = rows_buf.shape[0] // CHUNKS
    copies = []
    for at in range(CHUNKS):
        here = pl.ds(at * chunk, chunk)
        basis_buf[here, :] = lax.dot_general(
            rows_buf[here, :], solver, (((1,), (1,)), ((), ())), precision=EXACT, preferred_element_type=jnp.float32
        )
        copies.append(pltpu.make_async_copy(basis_buf.at[here], basis_ref.at[here], basis_sem.at[at]))
        copies[-1].start()
    for copy in copies:
        copy.wait()


def basis_and_factor(nodes, gram, rows):
    in_vmem = pl.BlockSpec(memory_space=pltpu.VMEM)
    in_hbm = pl.BlockSpec(memory_space=pltpu.HBM)
    return pl.pallas_call(
        functools.partial(factor_kernel, nodes),
        out_shape=(jax.ShapeDtypeStruct(rows.shape, jnp.float32), jax.ShapeDtypeStruct(gram.shape, jnp.float32)),
        in_specs=[in_vmem, in_hbm],
        out_specs=(in_hbm, in_vmem),
        input_output_aliases={1: 0},
        scratch_shapes=[
            pltpu.VMEM(rows.shape, jnp.float32),
            pltpu.VMEM(rows.shape, jnp.float32),
            pltpu.SemaphoreType.DMA,
            pltpu.SemaphoreType.DMA((CHUNKS,)),
        ],
        compiler_params=pltpu.CompilerParams(vmem_limit_bytes=16 << 20),
    )(gram, rows)


def device_groups(row_devices, col_devices, row_step, key):
    groups = {}
    for row, col in itertools.product(range(row_devices), range(col_devices)):
        groups.setdefault(key(row // row_step, row % row_step, col), []).append(row * col_devices + col)
    return list(groups.values())


def exchange(pieces, groups):
    return lax.all_to_all(pieces, ("rows", "cols"), 0, 0, axis_index_groups=groups, tiled=True)


def sum_over_devices(gram, row_devices, col_devices):
    row_step = 4
    plane = device_groups(row_devices, col_devices, row_step, lambda z, y, col: z)
    across = device_groups(row_devices, col_devices, row_step, lambda z, y, col: (y, col))
    in_plane, planes = len(plane[0]), len(across[0])
    size, width = gram.shape
    piece = exchange(gram.reshape(in_plane, size // in_plane, width), plane).sum(0)
    piece = exchange(jnp.broadcast_to(piece[None], (planes,) + piece.shape), across).sum(0)
    return exchange(jnp.broadcast_to(piece[None], (in_plane,) + piece.shape), plane).reshape(size, width)


def on_device(block_vector, op_tiles, tile_cols, live_counts):
    block_count, _, size, width = op_tiles.shape
    row_devices, col_devices = lax.axis_size("rows"), lax.axis_size("cols")
    rows_here = block_count * size
    rows_kept = block_count // col_devices

    def fetched_by(r, c):
        if c % 2 == 0:
            return (r, c + 1) if r == row_devices - 1 else (r + 1, c)
        return (r, c - 1) if r == 0 else (r - 1, c)

    steps = []
    for r, c in itertools.product(range(row_devices), range(col_devices)):
        to_r, to_c = fetched_by(r, c)
        steps.append((r * col_devices + c, to_r * col_devices + to_c))
    near = lax.ppermute(block_vector, ("rows", "cols"), steps)
    far = lax.ppermute(near, "cols", [(i, i ^ 1) for i in range(col_devices)])

    note = jnp.pad(tile_cols.reshape(1, 1, block_count).astype(jnp.float32), ((0, 0), (0, 0), (0, size - block_count)))
    note = jnp.broadcast_to(note, (col_devices, SUBLANES, size))
    sent = jnp.concatenate([op_tiles.reshape(col_devices, rows_kept * size, size), note], axis=1)
    sent = lax.all_to_all(sent, "cols", 0, 0, tiled=True)
    table = decode(live_counts.reshape(1, block_count), sent, rows_kept * size)
    part_rows, gram = product_and_gram(table, block_vector, sent, near, far, rows_kept, size)
    gram = sum_over_devices(gram, row_devices, col_devices)
    return basis_and_factor(rows_here * row_devices, gram, part_rows)


def solution(mesh):
    in_specs = (P("rows", None), P("rows", "cols", None, None), P("rows", "cols"), P("rows"))
    out_specs = (P(("rows", "cols"), None), P())
    return jax.shard_map(
        on_device, mesh=mesh, in_specs=in_specs, out_specs=out_specs, check_vma=False
    )
```

```python
import functools
import itertools

import jax
import jax.numpy as jnp
from jax import lax
from jax.experimental import pallas as pl
from jax.experimental.pallas import tpu as pltpu
from jax.sharding import PartitionSpec as P

EXACT = lax.Precision.HIGHEST
SUBLANES = 8
PANEL = 2
CHUNKS = 4


def split_bf16(x):
    high = x.astype(jnp.bfloat16)
    low = (x - high.astype(jnp.float32)).astype(jnp.bfloat16)
    return high, low


def product_kernel(
    count_ref, own_ref, sent_ref, near_ref, far_ref, out_ref, gram_ref,
    count_buf, note_buf, tile_buf, vec_buf, count_sem, note_sem, tile_sem, vec_sem,
):
    slots = sent_ref.shape[0]
    size, width = tile_buf.shape[2:]
    rows_kept = out_ref.shape[0] // size
    blocks = own_ref.shape[0] // size

    def copy_tiles(row):
        start = pl.multiple_of(row * size, size)
        return pltpu.make_async_copy(sent_ref.at[:, pl.ds(start, size)], tile_buf.at[row], tile_sem.at[row])

    def copy_vec(source, block, row, slot):
        start = pl.multiple_of(block * size, size)
        return pltpu.make_async_copy(source.at[pl.ds(start, size)], vec_buf.at[row, slot], vec_sem.at[row, slot])

    counts = pltpu.make_async_copy(count_ref, count_buf, count_sem)
    notes = pltpu.make_async_copy(sent_ref.at[:, pl.ds(rows_kept * size, 1)], note_buf, note_sem)
    counts.start()
    notes.start()
    copy_tiles(0).start()
    col = lax.axis_index("cols")
    kept_from, near_side = col * rows_kept, 2 * (col % 2)
    left_from = (lax.axis_index("rows") - 1) * blocks
    counts.wait()
    notes.wait()

    def count_of(row):
        return count_buf[kept_from + row]

    def fetch(row, carry):
        @pl.when(row > 0)
        def _():
            copy_tiles(row).start()

        def fetch_vec(slot, inner):
            block = note_buf[slot, 0, kept_from + row].astype(jnp.int32) - left_from
            side = (block >= blocks).astype(jnp.int32) + (block >= 2 * blocks).astype(jnp.int32)
            within = block - side * blocks

            @pl.when(side == 1)
            def _():
                copy_vec(own_ref, within, row, slot).start()

            @pl.when(side == near_side)
            def _():
                copy_vec(near_ref, within, row, slot).start()

            @pl.when(side == 2 - near_side)
            def _():
                copy_vec(far_ref, within, row, slot).start()

            return inner

        return lax.fori_loop(0, count_of(row), fetch_vec, carry)

    lax.fori_loop(0, rows_kept, fetch, 0)

    def row_block(row, carry):
        count = count_of(row)
        copy_tiles(row).wait()

        def wait_vec(slot, inner):
            copy_vec(own_ref, 0, row, slot).wait()
            return inner

        lax.fori_loop(0, count, wait_vec, 0)
        total = jnp.zeros((size, width), jnp.float32)
        for slot in range(0, slots, 2):
            pair = (slot, slot + 1)
            tiles = [tile_buf[row, one] for one in pair]
            vecs = [jnp.where(one < count, vec_buf[row, one], 0.0) for one in pair]
            tile_high, tile_low = split_bf16(jnp.concatenate(tiles, axis=1))
            vec_high, vec_low = split_bf16(jnp.concatenate(vecs, axis=0))
            both = jnp.dot(
                tile_high, jnp.concatenate([vec_high, vec_low], axis=1), preferred_element_type=jnp.float32
            )
            total += both[:, :width] + both[:, width:]
            total += jnp.dot(tile_low, vec_high, preferred_element_type=jnp.float32)
        out_ref[pl.ds(pl.multiple_of(row * size, size), size), :] = total
        return carry

    lax.fori_loop(0, rows_kept, row_block, 0)
    high, low = split_bf16(out_ref[...])
    both = jnp.concatenate([high, low], axis=1)
    gram = lax.dot_general(both, both, (((0,), (0,)), ((), ())), preferred_element_type=jnp.float32)
    gram_ref[...] = gram[:width, :width] + (gram[:width, width:] + gram[width:, :width]) + gram[width:, width:]


def hand_over_kernel(sent_ref, out_ref):
    pass


def hand_over(sent):
    return pl.pallas_call(
        hand_over_kernel,
        out_shape=jax.ShapeDtypeStruct(sent.shape, sent.dtype),
        in_specs=[pl.BlockSpec(memory_space=pl.ANY)],
        out_specs=pl.BlockSpec(memory_space=pl.ANY),
        input_output_aliases={0: 0},
        compiler_params=pltpu.CompilerParams(vmem_limit_bytes=62 << 20),
        cost_estimate=pl.CostEstimate(flops=1 << 33, bytes_accessed=1 << 26, transcendentals=0),
    )(sent)


def product_and_gram(counts, own, sent, near, far, rows_kept, size):
    slots, width = sent.shape[0], own.shape[1]
    in_vmem = pl.BlockSpec(memory_space=pltpu.VMEM)
    anywhere = pl.BlockSpec(memory_space=pl.ANY)
    return pl.pallas_call(
        product_kernel,
        out_shape=(
            jax.ShapeDtypeStruct((rows_kept * size, width), jnp.float32),
            jax.ShapeDtypeStruct((width, width), jnp.float32),
        ),
        in_specs=[anywhere] * 5,
        out_specs=(in_vmem, in_vmem),
        scratch_shapes=[
            pltpu.SMEM(counts.shape, jnp.int32),
            pltpu.SMEM((slots, 1, width), jnp.float32),
            pltpu.VMEM((rows_kept, slots, size, size), jnp.float32),
            pltpu.VMEM((rows_kept, slots, size, width), jnp.float32),
            pltpu.SemaphoreType.DMA,
            pltpu.SemaphoreType.DMA,
            pltpu.SemaphoreType.DMA((rows_kept,)),
            pltpu.SemaphoreType.DMA((rows_kept, slots)),
        ],
        compiler_params=pltpu.CompilerParams(vmem_limit_bytes=50 << 20),
    )(counts, own, sent, near, far)


def factor_kernel(nodes, gram_ref, rows_ref, basis_ref, factor_ref, basis_buf, basis_sem):
    size = gram_ref.shape[0]
    groups = size // SUBLANES
    shape = (SUBLANES, size)
    lane = lax.broadcasted_iota(jnp.int32, shape, 1)
    sub = lax.broadcasted_iota(jnp.int32, shape, 0)
    root = jnp.sqrt(jnp.float32(nodes))

    def column(x, at):
        return jnp.broadcast_to(x[:, at : at + 1], shape)

    def line(x, at):
        return jnp.broadcast_to(x[at : at + 1, :], shape)

    def total(terms):
        while len(terms) > 1:
            terms = [terms[i] + terms[i + 1] for i in range(0, len(terms), 2)]
        return terms[0]

    gram = [gram_ref[SUBLANES * i : SUBLANES * (i + 1), :] for i in range(groups)]
    inverse = [(lane == sub + SUBLANES * i).astype(jnp.float32) for i in range(groups)]
    for start in range(0, groups, PANEL):
        first = SUBLANES * start
        height = SUBLANES * PANEL
        rows = range(PANEL)
        x, v = gram[start : start + PANEL], inverse[start : start + PANEL]
        columns = [[column(x[q], first + i) for q in rows] for i in range(height)]
        upper, solved, pivots = list(x), list(v), [jnp.ones(shape) for q in rows]
        for i in range(height):
            at, within = divmod(i, SUBLANES)
            here = sub == within
            pivot = line(columns[i][at], within)
            x_line, v_line = line(x[at], within), line(v[at], within)
            upper[at], solved[at] = jnp.where(here, x_line, upper[at]), jnp.where(here, v_line, solved[at])
            pivots[at] = jnp.where(here, pivot, pivots[at])
            scale = 1.0 / pivot
            weight = [columns[i][q] * scale for q in rows]
            weight[at] = jnp.where(here, 0.0, weight[at])
            for q in rows:
                x[q], v[q] = x[q] - weight[q] * x_line, v[q] - weight[q] * v_line
            for j in range(i + 1, height):
                c_line = line(columns[j][at], within)
                for q in rows:
                    columns[j][q] = columns[j][q] - weight[q] * c_line
        x_lines, v_lines = [], []
        for q in rows:
            scale, norm, begin = 1.0 / pivots[q], lax.rsqrt(pivots[q]), first + SUBLANES * q
            factor_ref[begin : begin + SUBLANES, :] = jnp.where(lane >= sub + begin, upper[q] * norm, 0.0) / root
            inverse[start + q] = solved[q] * (norm * root)
            x[q], v[q] = x[q] * scale, v[q] * scale
            x_lines += [line(x[q], i) for i in range(SUBLANES)]
            v_lines += [line(v[q], i) for i in range(SUBLANES)]
        for below in range(start + PANEL, groups):
            weights = [column(gram[below], first + i) for i in range(height)]
            gram[below] = gram[below] - total([weights[i] * x_lines[i] for i in range(height)])
            inverse[below] = inverse[below] - total([weights[i] * v_lines[i] for i in range(height)])
    solver = jnp.concatenate(inverse, axis=0)
    chunk = rows_ref.shape[0] // CHUNKS
    copies = []
    for at in range(CHUNKS):
        here = pl.ds(at * chunk, chunk)
        basis_buf[here, :] = lax.dot_general(
            rows_ref[here, :], solver, (((1,), (1,)), ((), ())), precision=EXACT, preferred_element_type=jnp.float32
        )
        copies.append(pltpu.make_async_copy(basis_buf.at[here], basis_ref.at[here], basis_sem.at[at]))
        copies[-1].start()
    for copy in copies:
        copy.wait()


def basis_and_factor(nodes, gram, rows):
    in_vmem = pl.BlockSpec(memory_space=pltpu.VMEM)
    return pl.pallas_call(
        functools.partial(factor_kernel, nodes),
        out_shape=(jax.ShapeDtypeStruct(rows.shape, jnp.float32), jax.ShapeDtypeStruct(gram.shape, jnp.float32)),
        in_specs=[in_vmem, in_vmem],
        out_specs=(pl.BlockSpec(memory_space=pl.ANY), in_vmem),
        scratch_shapes=[
            pltpu.VMEM(rows.shape, jnp.float32),
            pltpu.SemaphoreType.DMA((CHUNKS,)),
        ],
        compiler_params=pltpu.CompilerParams(vmem_limit_bytes=16 << 20),
    )(gram, rows)


def device_groups(row_devices, col_devices, row_step, key):
    groups = {}
    for row, col in itertools.product(range(row_devices), range(col_devices)):
        groups.setdefault(key(row // row_step, row % row_step, col), []).append(row * col_devices + col)
    return list(groups.values())


def exchange(pieces, groups):
    return lax.all_to_all(pieces, ("rows", "cols"), 0, 0, axis_index_groups=groups, tiled=True)


def sum_over_devices(gram, row_devices, col_devices):
    row_step = 4
    plane = device_groups(row_devices, col_devices, row_step, lambda z, y, col: z)
    across = device_groups(row_devices, col_devices, row_step, lambda z, y, col: (y, col))
    in_plane, planes = len(plane[0]), len(across[0])
    size, width = gram.shape
    piece = exchange(gram.reshape(in_plane, size // in_plane, width), plane).sum(0)
    piece = exchange(jnp.broadcast_to(piece[None], (planes,) + piece.shape), across).sum(0)
    return exchange(jnp.broadcast_to(piece[None], (in_plane,) + piece.shape), plane).reshape(size, width)


def on_device(block_vector, op_tiles, tile_cols, live_counts):
    block_count, _, size, width = op_tiles.shape
    row_devices, col_devices = lax.axis_size("rows"), lax.axis_size("cols")
    rows_here = block_count * size
    rows_kept = block_count // col_devices

    def fetched_by(r, c):
        if c % 2 == 0:
            return (r, c + 1) if r == row_devices - 1 else (r + 1, c)
        return (r, c - 1) if r == 0 else (r - 1, c)

    steps = []
    for r, c in itertools.product(range(row_devices), range(col_devices)):
        to_r, to_c = fetched_by(r, c)
        steps.append((r * col_devices + c, to_r * col_devices + to_c))
    near = lax.ppermute(block_vector, ("rows", "cols"), steps)
    far = lax.ppermute(near, "cols", [(i, i ^ 1) for i in range(col_devices)])

    note = jnp.pad(tile_cols.reshape(1, 1, block_count).astype(jnp.float32), ((0, 0), (0, 0), (0, size - block_count)))
    note = jnp.broadcast_to(note, (col_devices, SUBLANES, size))
    sent = jnp.concatenate([op_tiles.reshape(col_devices, rows_kept * size, size), note], axis=1)
    sent = lax.all_to_all(sent, "cols", 0, 0, tiled=True)
    part_rows, gram = product_and_gram(live_counts, block_vector, hand_over(sent), near, far, rows_kept, size)
    gram = sum_over_devices(gram, row_devices, col_devices)
    return basis_and_factor(rows_here * row_devices, gram, part_rows)


def solution(mesh):
    in_specs = (P("rows", None), P("rows", "cols", None, None), P("rows", "cols"), P("rows"))
    out_specs = (P(("rows", "cols"), None), P())
    return jax.shard_map(
        on_device, mesh=mesh, in_specs=in_specs, out_specs=out_specs, check_vma=False
    )
```

```python
import functools
import itertools

import jax
import jax.numpy as jnp
from jax import lax
from jax.experimental import pallas as pl
from jax.experimental.pallas import tpu as pltpu
from jax.sharding import PartitionSpec as P

EXACT = lax.Precision.HIGHEST
SUBLANES = 8
PANEL = 2
CHUNKS = 4


def split_bf16(x):
    high = x.astype(jnp.bfloat16)
    low = (x - high.astype(jnp.float32)).astype(jnp.bfloat16)
    return high, low


def product_kernel(
    count_ref, own_ref, sent_ref, near_ref, far_ref, out_ref, gram_ref,
    count_buf, note_buf, tile_buf, vec_buf, count_sem, note_sem, tile_sem, vec_sem,
):
    slots = sent_ref.shape[0]
    size, width = tile_buf.shape[2:]
    rows_kept = out_ref.shape[0] // size
    blocks = own_ref.shape[0] // size

    def copy_tiles(row):
        start = pl.multiple_of(row * size, size)
        return pltpu.make_async_copy(sent_ref.at[:, pl.ds(start, size)], tile_buf.at[row], tile_sem.at[row])

    def copy_vec(source, block, row, slot):
        start = pl.multiple_of(block * size, size)
        return pltpu.make_async_copy(source.at[pl.ds(start, size)], vec_buf.at[row, slot], vec_sem.at[row, slot])

    counts = pltpu.make_async_copy(count_ref, count_buf, count_sem)
    notes = pltpu.make_async_copy(sent_ref.at[:, pl.ds(rows_kept * size, 1)], note_buf, note_sem)
    counts.start()
    notes.start()
    copy_tiles(0).start()
    col = lax.axis_index("cols")
    kept_from, near_side = col * rows_kept, 2 * (col % 2)
    left_from = (lax.axis_index("rows") - 1) * blocks
    counts.wait()
    notes.wait()

    def count_of(row):
        return count_buf[kept_from + row]

    def fetch(row, carry):
        @pl.when(row > 0)
        def _():
            copy_tiles(row).start()

        def fetch_vec(slot, inner):
            block = note_buf[slot, 0, kept_from + row].astype(jnp.int32) - left_from
            side = (block >= blocks).astype(jnp.int32) + (block >= 2 * blocks).astype(jnp.int32)
            within = block - side * blocks

            @pl.when(side == 1)
            def _():
                copy_vec(own_ref, within, row, slot).start()

            @pl.when(side == near_side)
            def _():
                copy_vec(near_ref, within, row, slot).start()

            @pl.when(side == 2 - near_side)
            def _():
                copy_vec(far_ref, within, row, slot).start()

            return inner

        return lax.fori_loop(0, count_of(row), fetch_vec, carry)

    lax.fori_loop(0, rows_kept, fetch, 0)

    def row_block(row, carry):
        count = count_of(row)
        copy_tiles(row).wait()

        def wait_vec(slot, inner):
            copy_vec(own_ref, 0, row, slot).wait()
            return inner

        lax.fori_loop(0, count, wait_vec, 0)
        total = jnp.zeros((size, width), jnp.float32)
        for slot in range(0, slots, 2):
            pair = (slot, slot + 1)
            tiles = [tile_buf[row, one] for one in pair]
            vecs = [jnp.where(one < count, vec_buf[row, one], 0.0) for one in pair]
            tile_high, tile_low = split_bf16(jnp.concatenate(tiles, axis=1))
            vec_high, vec_low = split_bf16(jnp.concatenate(vecs, axis=0))
            both = jnp.dot(
                tile_high, jnp.concatenate([vec_high, vec_low], axis=1), preferred_element_type=jnp.float32
            )
            total += both[:, :width] + both[:, width:]
            total += jnp.dot(tile_low, vec_high, preferred_element_type=jnp.float32)
        out_ref[pl.ds(pl.multiple_of(row * size, size), size), :] = total
        return carry

    lax.fori_loop(0, rows_kept, row_block, 0)
    high, low = split_bf16(out_ref[...])
    both = jnp.concatenate([high, low], axis=1)
    gram = lax.dot_general(both, both, (((0,), (0,)), ((), ())), preferred_element_type=jnp.float32)
    gram_ref[...] = gram[:width, :width] + (gram[:width, width:] + gram[width:, :width]) + gram[width:, width:]


def hand_over_kernel(sent_ref, out_ref):
    pass


def hand_over(sent):
    return pl.pallas_call(
        hand_over_kernel,
        out_shape=jax.ShapeDtypeStruct(sent.shape, sent.dtype),
        in_specs=[pl.BlockSpec(memory_space=pl.ANY)],
        out_specs=pl.BlockSpec(memory_space=pl.ANY),
        input_output_aliases={0: 0},
        compiler_params=pltpu.CompilerParams(vmem_limit_bytes=62 << 20),
        cost_estimate=pl.CostEstimate(flops=1 << 33, bytes_accessed=1 << 26, transcendentals=0),
    )(sent)


def product_and_gram(counts, own, sent, near, far, rows_kept, size):
    slots, width = sent.shape[0], own.shape[1]
    in_vmem = pl.BlockSpec(memory_space=pltpu.VMEM)
    anywhere = pl.BlockSpec(memory_space=pl.ANY)
    return pl.pallas_call(
        product_kernel,
        out_shape=(
            jax.ShapeDtypeStruct((rows_kept * size, width), jnp.float32),
            jax.ShapeDtypeStruct((width, width), jnp.float32),
        ),
        in_specs=[anywhere] * 5,
        out_specs=(in_vmem, in_vmem),
        scratch_shapes=[
            pltpu.SMEM(counts.shape, jnp.int32),
            pltpu.SMEM((slots, 1, width), jnp.float32),
            pltpu.VMEM((rows_kept, slots, size, size), jnp.float32),
            pltpu.VMEM((rows_kept, slots, size, width), jnp.float32),
            pltpu.SemaphoreType.DMA,
            pltpu.SemaphoreType.DMA,
            pltpu.SemaphoreType.DMA((rows_kept,)),
            pltpu.SemaphoreType.DMA((rows_kept, slots)),
        ],
        compiler_params=pltpu.CompilerParams(vmem_limit_bytes=50 << 20),
    )(counts, own, sent, near, far)


def factor_kernel(nodes, gram_ref, rows_ref, basis_ref, factor_ref, basis_buf, basis_sem):
    size = gram_ref.shape[0]
    groups = size // SUBLANES
    shape = (SUBLANES, size)
    lane = lax.broadcasted_iota(jnp.int32, shape, 1)
    sub = lax.broadcasted_iota(jnp.int32, shape, 0)
    root = jnp.sqrt(jnp.float32(nodes))

    def column(x, at):
        return jnp.broadcast_to(x[:, at : at + 1], shape)

    def line(x, at):
        return jnp.broadcast_to(x[at : at + 1, :], shape)

    def total(terms):
        while len(terms) > 1:
            terms = [terms[i] + terms[i + 1] for i in range(0, len(terms), 2)]
        return terms[0]

    gram = [gram_ref[SUBLANES * i : SUBLANES * (i + 1), :] for i in range(groups)]
    inverse = [(lane == sub + SUBLANES * i).astype(jnp.float32) for i in range(groups)]
    for start in range(0, groups, PANEL):
        first = SUBLANES * start
        height = SUBLANES * PANEL
        rows = range(PANEL)
        x, v = gram[start : start + PANEL], inverse[start : start + PANEL]
        columns = [[column(x[q], first + i) for q in rows] for i in range(height)]
        upper, solved, pivots = list(x), list(v), [jnp.ones(shape) for q in rows]
        for i in range(height):
            at, within = divmod(i, SUBLANES)
            here = sub == within
            pivot = line(columns[i][at], within)
            x_line, v_line = line(x[at], within), line(v[at], within)
            upper[at], solved[at] = jnp.where(here, x_line, upper[at]), jnp.where(here, v_line, solved[at])
            pivots[at] = jnp.where(here, pivot, pivots[at])
            scale = 1.0 / pivot
            weight = [columns[i][q] * scale for q in rows]
            weight[at] = jnp.where(here, 0.0, weight[at])
            for q in rows:
                x[q], v[q] = x[q] - weight[q] * x_line, v[q] - weight[q] * v_line
            for j in range(i + 1, height):
                c_line = line(columns[j][at], within)
                for q in rows:
                    columns[j][q] = columns[j][q] - weight[q] * c_line
        x_lines, v_lines = [], []
        for q in rows:
            scale, norm, begin = 1.0 / pivots[q], lax.rsqrt(pivots[q]), first + SUBLANES * q
            factor_ref[begin : begin + SUBLANES, :] = jnp.where(lane >= sub + begin, upper[q] * norm, 0.0) / root
            inverse[start + q] = solved[q] * (norm * root)
            x[q], v[q] = x[q] * scale, v[q] * scale
            x_lines += [line(x[q], i) for i in range(SUBLANES)]
            v_lines += [line(v[q], i) for i in range(SUBLANES)]
        for below in range(start + PANEL, groups):
            weights = [column(gram[below], first + i) for i in range(height)]
            gram[below] = gram[below] - total([weights[i] * x_lines[i] for i in range(height)])
            inverse[below] = inverse[below] - total([weights[i] * v_lines[i] for i in range(height)])
    solver = jnp.concatenate(inverse, axis=0)
    chunk = rows_ref.shape[0] // CHUNKS
    copies = []
    for at in range(CHUNKS):
        here = pl.ds(at * chunk, chunk)
        basis_buf[here, :] = lax.dot_general(
            rows_ref[here, :], solver, (((1,), (1,)), ((), ())), precision=EXACT, preferred_element_type=jnp.float32
        )
        copies.append(pltpu.make_async_copy(basis_buf.at[here], basis_ref.at[here], basis_sem.at[at]))
        copies[-1].start()
    for copy in copies:
        copy.wait()


def basis_and_factor(nodes, gram, rows):
    in_vmem = pl.BlockSpec(memory_space=pltpu.VMEM)
    return pl.pallas_call(
        functools.partial(factor_kernel, nodes),
        out_shape=(jax.ShapeDtypeStruct(rows.shape, jnp.float32), jax.ShapeDtypeStruct(gram.shape, jnp.float32)),
        in_specs=[in_vmem, in_vmem],
        out_specs=(pl.BlockSpec(memory_space=pl.ANY), in_vmem),
        scratch_shapes=[
            pltpu.VMEM(rows.shape, jnp.float32),
            pltpu.SemaphoreType.DMA((CHUNKS,)),
        ],
        compiler_params=pltpu.CompilerParams(vmem_limit_bytes=16 << 20),
    )(gram, rows)


def device_groups(row_devices, col_devices, row_step, key):
    groups = {}
    for row, col in itertools.product(range(row_devices), range(col_devices)):
        groups.setdefault(key(row // row_step, row % row_step, col), []).append(row * col_devices + col)
    return list(groups.values())


def exchange(pieces, groups):
    return lax.all_to_all(pieces, ("rows", "cols"), 0, 0, axis_index_groups=groups, tiled=True)


def sum_over_devices(gram, row_devices, col_devices):
    row_step = 4
    plane = device_groups(row_devices, col_devices, row_step, lambda z, y, col: z)
    across = device_groups(row_devices, col_devices, row_step, lambda z, y, col: (y, col))
    in_plane, planes = len(plane[0]), len(across[0])
    size, width = gram.shape
    piece = exchange(gram.reshape(in_plane, size // in_plane, width), plane).sum(0)
    piece = exchange(jnp.broadcast_to(piece[None], (planes,) + piece.shape), across).sum(0)
    return exchange(jnp.broadcast_to(piece[None], (in_plane,) + piece.shape), plane).reshape(size, width)


def on_device(block_vector, op_tiles, tile_cols, live_counts):
    block_count, _, size, width = op_tiles.shape
    row_devices, col_devices = lax.axis_size("rows"), lax.axis_size("cols")
    rows_here = block_count * size
    rows_kept = block_count // col_devices

    def fetched_by(r, c):
        if c % 2 == 0:
            return (r, c + 1) if r == row_devices - 1 else (r + 1, c)
        return (r, c - 1) if r == 0 else (r - 1, c)

    steps = []
    for r, c in itertools.product(range(row_devices), range(col_devices)):
        to_r, to_c = fetched_by(r, c)
        steps.append((r * col_devices + c, to_r * col_devices + to_c))
    note = jnp.pad(tile_cols.reshape(1, 1, block_count).astype(jnp.float32), ((0, 0), (0, 0), (0, size - block_count)))
    note = jnp.broadcast_to(note, (col_devices, SUBLANES, size))
    sent = jnp.concatenate([op_tiles.reshape(col_devices, rows_kept * size, size), note], axis=1)
    source, sent = lax.optimization_barrier((block_vector, sent))
    near = lax.ppermute(source, ("rows", "cols"), steps)
    far = lax.ppermute(near, "cols", [(i, i ^ 1) for i in range(col_devices)])
    sent = lax.all_to_all(sent, "cols", 0, 0, tiled=True)
    part_rows, gram = product_and_gram(live_counts, block_vector, hand_over(sent), near, far, rows_kept, size)
    gram = sum_over_devices(gram, row_devices, col_devices)
    return basis_and_factor(rows_here * row_devices, gram, part_rows)


def solution(mesh):
    in_specs = (P("rows", None), P("rows", "cols", None, None), P("rows", "cols"), P("rows"))
    out_specs = (P(("rows", "cols"), None), P())
    return jax.shard_map(
        on_device, mesh=mesh, in_specs=in_specs, out_specs=out_specs, check_vma=False
    )
```

```python
import functools
import itertools

import jax
import jax.numpy as jnp
from jax import lax
from jax.experimental import pallas as pl
from jax.experimental.pallas import tpu as pltpu
from jax.sharding import PartitionSpec as P

EXACT = lax.Precision.HIGHEST
SUBLANES = 8
PANEL = 2
CHUNKS = 4


def split_bf16(x):
    high = x.astype(jnp.bfloat16)
    low = (x - high.astype(jnp.float32)).astype(jnp.bfloat16)
    return high, low


def product_kernel(
    count_ref, own_ref, sent_ref, near_ref, far_ref, out_ref, gram_ref,
    count_buf, note_buf, tile_buf, vec_buf, count_sem, note_sem, tile_sem, vec_sem,
):
    slots = sent_ref.shape[0]
    size, width = tile_buf.shape[2:]
    rows_kept = out_ref.shape[0] // size
    blocks = own_ref.shape[0] // size

    def copy_tiles(row):
        start = pl.multiple_of(row * size, size)
        return pltpu.make_async_copy(sent_ref.at[:, pl.ds(start, size)], tile_buf.at[row], tile_sem.at[row])

    def copy_vec(source, block, row, slot):
        start = pl.multiple_of(block * size, size)
        return pltpu.make_async_copy(source.at[pl.ds(start, size)], vec_buf.at[row, slot], vec_sem.at[row, slot])

    counts = pltpu.make_async_copy(count_ref, count_buf, count_sem)
    notes = pltpu.make_async_copy(sent_ref.at[:, pl.ds(rows_kept * size, 1)], note_buf, note_sem)
    counts.start()
    notes.start()
    copy_tiles(0).start()
    col = lax.axis_index("cols")
    kept_from, near_side = col * rows_kept, 2 * (col % 2)
    left_from = (lax.axis_index("rows") - 1) * blocks
    counts.wait()
    notes.wait()

    def count_of(row):
        return count_buf[kept_from + row]

    def fetch(row, carry):
        @pl.when(row > 0)
        def _():
            copy_tiles(row).start()

        def fetch_vec(slot, inner):
            block = note_buf[slot, 0, kept_from + row].astype(jnp.int32) - left_from
            side = (block >= blocks).astype(jnp.int32) + (block >= 2 * blocks).astype(jnp.int32)
            within = block - side * blocks

            @pl.when(side == 1)
            def _():
                copy_vec(own_ref, within, row, slot).start()

            @pl.when(side == near_side)
            def _():
                copy_vec(near_ref, within, row, slot).start()

            @pl.when(side == 2 - near_side)
            def _():
                copy_vec(far_ref, within, row, slot).start()

            return inner

        return lax.fori_loop(0, count_of(row), fetch_vec, carry)

    lax.fori_loop(0, rows_kept, fetch, 0)

    def row_block(row, carry):
        count = count_of(row)
        copy_tiles(row).wait()

        def wait_vec(slot, inner):
            copy_vec(own_ref, 0, row, slot).wait()
            return inner

        lax.fori_loop(0, count, wait_vec, 0)
        total = jnp.zeros((size, width), jnp.float32)
        for slot in range(0, slots, 2):
            pair = (slot, slot + 1)
            tiles = [tile_buf[row, one] for one in pair]
            vecs = [jnp.where(one < count, vec_buf[row, one], 0.0) for one in pair]
            tile_high, tile_low = split_bf16(jnp.concatenate(tiles, axis=1))
            vec_high, vec_low = split_bf16(jnp.concatenate(vecs, axis=0))
            both = jnp.dot(
                tile_high, jnp.concatenate([vec_high, vec_low], axis=1), preferred_element_type=jnp.float32
            )
            total += both[:, :width] + both[:, width:]
            total += jnp.dot(tile_low, vec_high, preferred_element_type=jnp.float32)
        out_ref[pl.ds(pl.multiple_of(row * size, size), size), :] = total
        return carry

    lax.fori_loop(0, rows_kept, row_block, 0)
    high, low = split_bf16(out_ref[...])
    both = jnp.concatenate([high, low], axis=1)
    gram = lax.dot_general(both, both, (((0,), (0,)), ((), ())), preferred_element_type=jnp.float32)
    gram_ref[...] = gram[:width, :width] + (gram[:width, width:] + gram[width:, :width]) + gram[width:, width:]


def pack_kernel(tile_ref, number_ref, out_ref, tile_buf, note_buf, in_sem, out_sem, note_sem):
    slots, rows, _ = tile_ref.shape
    arrive = [pltpu.make_async_copy(tile_ref.at[at], tile_buf.at[at], in_sem.at[at]) for at in range(slots)]
    leave = [
        pltpu.make_async_copy(tile_buf.at[at], out_ref.at[at, pl.ds(0, rows)], out_sem.at[at]) for at in range(slots)
    ]
    for copy in arrive:
        copy.start()
    blocks = number_ref.shape[1]
    note_buf[...] = jnp.zeros_like(note_buf)
    note_buf[:, :, :blocks] = jnp.broadcast_to(number_ref[...].astype(jnp.float32)[None], (slots, SUBLANES, blocks))
    note = pltpu.make_async_copy(note_buf, out_ref.at[:, pl.ds(rows, SUBLANES)], note_sem)
    note.start()
    for at in range(slots):
        arrive[at].wait()
        leave[at].start()
    for copy in leave:
        copy.wait()
    note.wait()


def pack(tiles, numbers):
    slots, rows, size = tiles.shape
    return pl.pallas_call(
        pack_kernel,
        out_shape=jax.ShapeDtypeStruct((slots, rows + SUBLANES, size), jnp.float32),
        in_specs=[pl.BlockSpec(memory_space=pl.ANY), pl.BlockSpec(memory_space=pltpu.VMEM)],
        out_specs=pl.BlockSpec(memory_space=pl.ANY),
        scratch_shapes=[
            pltpu.VMEM(tiles.shape, jnp.float32),
            pltpu.VMEM((slots, SUBLANES, size), jnp.float32),
            pltpu.SemaphoreType.DMA((slots,)),
            pltpu.SemaphoreType.DMA((slots,)),
            pltpu.SemaphoreType.DMA,
        ],
        compiler_params=pltpu.CompilerParams(vmem_limit_bytes=62 << 20),
        cost_estimate=pl.CostEstimate(flops=0, bytes_accessed=8 << 20, transcendentals=0),
    )(tiles, numbers)


def hand_over_kernel(sent_ref, out_ref):
    pass


def hand_over(sent):
    return pl.pallas_call(
        hand_over_kernel,
        out_shape=jax.ShapeDtypeStruct(sent.shape, sent.dtype),
        in_specs=[pl.BlockSpec(memory_space=pl.ANY)],
        out_specs=pl.BlockSpec(memory_space=pl.ANY),
        input_output_aliases={0: 0},
        compiler_params=pltpu.CompilerParams(vmem_limit_bytes=62 << 20),
        cost_estimate=pl.CostEstimate(flops=1 << 33, bytes_accessed=1 << 26, transcendentals=0),
    )(sent)


def product_and_gram(counts, own, sent, near, far, rows_kept, size):
    slots, width = sent.shape[0], own.shape[1]
    in_vmem = pl.BlockSpec(memory_space=pltpu.VMEM)
    anywhere = pl.BlockSpec(memory_space=pl.ANY)
    return pl.pallas_call(
        product_kernel,
        out_shape=(
            jax.ShapeDtypeStruct((rows_kept * size, width), jnp.float32),
            jax.ShapeDtypeStruct((width, width), jnp.float32),
        ),
        in_specs=[anywhere] * 5,
        out_specs=(in_vmem, in_vmem),
        scratch_shapes=[
            pltpu.SMEM(counts.shape, jnp.int32),
            pltpu.SMEM((slots, 1, width), jnp.float32),
            pltpu.VMEM((rows_kept, slots, size, size), jnp.float32),
            pltpu.VMEM((rows_kept, slots, size, width), jnp.float32),
            pltpu.SemaphoreType.DMA,
            pltpu.SemaphoreType.DMA,
            pltpu.SemaphoreType.DMA((rows_kept,)),
            pltpu.SemaphoreType.DMA((rows_kept, slots)),
        ],
        compiler_params=pltpu.CompilerParams(vmem_limit_bytes=50 << 20),
    )(counts, own, sent, near, far)


def factor_kernel(nodes, gram_ref, rows_ref, basis_ref, factor_ref, basis_buf, basis_sem):
    size = gram_ref.shape[0]
    groups = size // SUBLANES
    shape = (SUBLANES, size)
    lane = lax.broadcasted_iota(jnp.int32, shape, 1)
    sub = lax.broadcasted_iota(jnp.int32, shape, 0)
    root = jnp.sqrt(jnp.float32(nodes))

    def column(x, at):
        return jnp.broadcast_to(x[:, at : at + 1], shape)

    def line(x, at):
        return jnp.broadcast_to(x[at : at + 1, :], shape)

    def total(terms):
        while len(terms) > 1:
            terms = [terms[i] + terms[i + 1] for i in range(0, len(terms), 2)]
        return terms[0]

    gram = [gram_ref[SUBLANES * i : SUBLANES * (i + 1), :] for i in range(groups)]
    inverse = [(lane == sub + SUBLANES * i).astype(jnp.float32) for i in range(groups)]
    for start in range(0, groups, PANEL):
        first = SUBLANES * start
        height = SUBLANES * PANEL
        rows = range(PANEL)
        x, v = gram[start : start + PANEL], inverse[start : start + PANEL]
        columns = [[column(x[q], first + i) for q in rows] for i in range(height)]
        upper, solved, pivots = list(x), list(v), [jnp.ones(shape) for q in rows]
        for i in range(height):
            at, within = divmod(i, SUBLANES)
            here = sub == within
            pivot = line(columns[i][at], within)
            x_line, v_line = line(x[at], within), line(v[at], within)
            upper[at], solved[at] = jnp.where(here, x_line, upper[at]), jnp.where(here, v_line, solved[at])
            pivots[at] = jnp.where(here, pivot, pivots[at])
            scale = 1.0 / pivot
            weight = [columns[i][q] * scale for q in rows]
            weight[at] = jnp.where(here, 0.0, weight[at])
            for q in rows:
                x[q], v[q] = x[q] - weight[q] * x_line, v[q] - weight[q] * v_line
            for j in range(i + 1, height):
                c_line = line(columns[j][at], within)
                for q in rows:
                    columns[j][q] = columns[j][q] - weight[q] * c_line
        x_lines, v_lines = [], []
        for q in rows:
            scale, norm, begin = 1.0 / pivots[q], lax.rsqrt(pivots[q]), first + SUBLANES * q
            factor_ref[begin : begin + SUBLANES, :] = jnp.where(lane >= sub + begin, upper[q] * norm, 0.0) / root
            inverse[start + q] = solved[q] * (norm * root)
            x[q], v[q] = x[q] * scale, v[q] * scale
            x_lines += [line(x[q], i) for i in range(SUBLANES)]
            v_lines += [line(v[q], i) for i in range(SUBLANES)]
        for below in range(start + PANEL, groups):
            weights = [column(gram[below], first + i) for i in range(height)]
            gram[below] = gram[below] - total([weights[i] * x_lines[i] for i in range(height)])
            inverse[below] = inverse[below] - total([weights[i] * v_lines[i] for i in range(height)])
    solver = jnp.concatenate(inverse, axis=0)
    chunk = rows_ref.shape[0] // CHUNKS
    copies = []
    for at in range(CHUNKS):
        here = pl.ds(at * chunk, chunk)
        basis_buf[here, :] = lax.dot_general(
            rows_ref[here, :], solver, (((1,), (1,)), ((), ())), precision=EXACT, preferred_element_type=jnp.float32
        )
        copies.append(pltpu.make_async_copy(basis_buf.at[here], basis_ref.at[here], basis_sem.at[at]))
        copies[-1].start()
    for copy in copies:
        copy.wait()


def basis_and_factor(nodes, gram, rows):
    in_vmem = pl.BlockSpec(memory_space=pltpu.VMEM)
    return pl.pallas_call(
        functools.partial(factor_kernel, nodes),
        out_shape=(jax.ShapeDtypeStruct(rows.shape, jnp.float32), jax.ShapeDtypeStruct(gram.shape, jnp.float32)),
        in_specs=[in_vmem, in_vmem],
        out_specs=(pl.BlockSpec(memory_space=pl.ANY), in_vmem),
        scratch_shapes=[
            pltpu.VMEM(rows.shape, jnp.float32),
            pltpu.SemaphoreType.DMA((CHUNKS,)),
        ],
        compiler_params=pltpu.CompilerParams(vmem_limit_bytes=16 << 20),
    )(gram, rows)


def device_groups(row_devices, col_devices, row_step, key):
    groups = {}
    for row, col in itertools.product(range(row_devices), range(col_devices)):
        groups.setdefault(key(row // row_step, row % row_step, col), []).append(row * col_devices + col)
    return list(groups.values())


def exchange(pieces, groups):
    return lax.all_to_all(pieces, ("rows", "cols"), 0, 0, axis_index_groups=groups, tiled=True)


def sum_over_devices(gram, row_devices, col_devices):
    row_step = 4
    plane = device_groups(row_devices, col_devices, row_step, lambda z, y, col: z)
    across = device_groups(row_devices, col_devices, row_step, lambda z, y, col: (y, col))
    in_plane, planes = len(plane[0]), len(across[0])
    size, width = gram.shape
    piece = exchange(gram.reshape(in_plane, size // in_plane, width), plane).sum(0)
    piece = exchange(jnp.broadcast_to(piece[None], (planes,) + piece.shape), across).sum(0)
    return exchange(jnp.broadcast_to(piece[None], (in_plane,) + piece.shape), plane).reshape(size, width)


def on_device(block_vector, op_tiles, tile_cols, live_counts):
    block_count, _, size, width = op_tiles.shape
    row_devices, col_devices = lax.axis_size("rows"), lax.axis_size("cols")
    rows_here = block_count * size
    rows_kept = block_count // col_devices

    def fetched_by(r, c):
        if c % 2 == 0:
            return (r, c + 1) if r == row_devices - 1 else (r + 1, c)
        return (r, c - 1) if r == 0 else (r - 1, c)

    steps = []
    for r, c in itertools.product(range(row_devices), range(col_devices)):
        to_r, to_c = fetched_by(r, c)
        steps.append((r * col_devices + c, to_r * col_devices + to_c))
    near = lax.ppermute(block_vector, ("rows", "cols"), steps)
    far = lax.ppermute(near, "cols", [(i, i ^ 1) for i in range(col_devices)])

    sent = pack(op_tiles.reshape(col_devices, rows_kept * size, size), tile_cols.reshape(1, block_count))
    sent = lax.all_to_all(sent, "cols", 0, 0, tiled=True)
    part_rows, gram = product_and_gram(live_counts, block_vector, hand_over(sent), near, far, rows_kept, size)
    gram = sum_over_devices(gram, row_devices, col_devices)
    return basis_and_factor(rows_here * row_devices, gram, part_rows)


def solution(mesh):
    in_specs = (P("rows", None), P("rows", "cols", None, None), P("rows", "cols"), P("rows"))
    out_specs = (P(("rows", "cols"), None), P())
    return jax.shard_map(
        on_device, mesh=mesh, in_specs=in_specs, out_specs=out_specs, check_vma=False
    )
```
